256 devices in a mesh: rec: 2 (over core), tm: 128 (over y, x, z).
Axes of the slice: x: 4, y: 4, z: 8, core: 2. Of those that a mesh axis runs over, the one named last changes fastest.
Arguments:
- frames: bfloat16 [2, 131072, 1280], P('rec', 'tm'), may hold values from -6 to 6
- segments: int32 [2, 256, 2], P('rec'), may hold values from 0 to 131072, as said below
- ln_gain: float32 [1280], replicated, may hold values from 0.5 to 6
- w_query: bfloat16 [1280, 640], replicated, may hold values from -0.15625 to 0.15625
- w_key: bfloat16 [1280, 640], replicated, may hold values from -0.15625 to 0.15625
- w_value: bfloat16 [1280, 640], replicated, may hold values from -0.15625 to 0.15625
- w_out: bfloat16 [640, 1280], replicated, may hold values from -0.25 to 0.25
- conv_gain: float32 [1280], replicated, may hold values from 0.5 to 1.5
- conv_weight: float32 [31, 1280], replicated, may hold values from -1 to 1
Outputs:
- layer_out: bfloat16 [2, 131072, 1280], P('rec', 'tm')
The draws below stay inside these ranges and needn't reach their ends.
Inputs may be any that keep to these rules, and one draw needn't show every extreme that they name: `segments`: per recording, 256 pairs [start, end) of multiples of 128, increasing, with 128 or more frames between one end and the next start; the first starts at 0, the last ends at 131072, half of the frames lie inside pairs, and one pair covers frames 131072 // 2 - 1024 to 65536.
All inputs are finite; a program needn't handle non-finite values.
Results may differ from the reference program's by a relative error of at most 0.0059.
The reference program's roundings to bfloat16 on the way (of `normed`, `query`, `probs`, `heads_out` and `conv_in`) count: a program that leaves them out, or rounds other values in their place, can miss the bound.
Values may be sent and summed in bfloat16 or wider, within the bound.
No kernel may reach another device: no remote copies, remote signals or barrier semaphores. Data moves between devices by JAX's collectives and lax.ppermute only.
A program may use at most 128 MiB of HBM per device.

```python
import jax
import jax.numpy as jnp
from jax import lax

D = 1280
H = 10
HS = 64
CTX = 256
KSZ = 31
F_DEV = 1024
HD = 640
RECS = 2
FRAMES = 131072
SEGS = 256


def half_list(key, n_blocks, n_segs, tail_blocks):
    talk = n_blocks // 2
    quiet = n_blocks - talk
    longs = max(1, n_segs // 32)
    key_runs, key_base, key_pick, key_share = jax.random.split(key, 4)
    extra = talk - n_segs - (tail_blocks - 1)
    places = extra + n_segs - 1
    cuts = jnp.sort(jax.random.permutation(key_runs, places)[:n_segs - 1]).astype(jnp.int32)
    edges = jnp.concatenate([jnp.full((1,), -1, jnp.int32), cuts, jnp.full((1,), places, jnp.int32)])
    runs = (edges[1:] - edges[:-1]).astype(jnp.int32)
    runs = runs + jnp.concatenate([jnp.zeros((n_segs - 1,), jnp.int32), jnp.full((1,), tail_blocks - 1, jnp.int32)])
    base = 1 + jax.random.randint(key_base, (n_segs - 1,), 0, 2, jnp.int32)
    remain = quiet - jnp.sum(base)
    weights = jax.random.randint(key_share, (longs,), 1, 8, jnp.int32)
    marks = jnp.concatenate([jnp.zeros((1,), jnp.int32), jnp.cumsum(weights)])
    shares = remain * marks // marks[-1]
    parts = (shares[1:] - shares[:-1]).astype(jnp.int32)
    chosen = jax.random.permutation(key_pick, n_segs - 1)[:longs].astype(jnp.int32)
    slots = jnp.arange(n_segs - 1, dtype=jnp.int32)
    gaps = base + jnp.sum(jnp.where(slots[:, None] == chosen[None, :], parts[None, :], 0), axis=1).astype(jnp.int32)
    cycle = runs + jnp.concatenate([gaps, jnp.zeros((1,), jnp.int32)])
    starts = (jnp.cumsum(cycle) - cycle).astype(jnp.int32)
    ends = starts + runs
    return (starts, ends)


def one_list(key):
    half_blocks = FRAMES // 256
    first_segs = SEGS // 2
    key_a, key_b = jax.random.split(key, 2)
    starts_a, ends_a = half_list(key_a, half_blocks, first_segs, F_DEV // 128)
    starts_b, ends_b = half_list(key_b, half_blocks, SEGS - first_segs + 1, 1)
    starts_b = starts_b + half_blocks
    ends_b = ends_b + half_blocks
    starts = jnp.concatenate([starts_a, starts_b[1:]])
    ends = jnp.concatenate([ends_a[:-1], ends_b])
    return (jnp.stack([starts, ends], axis=-1) * 128).astype(jnp.int32)


def draw_segments(key, part):
    key = jax.random.fold_in(key, 1)
    keys = jax.random.split(key, RECS)
    return jax.vmap(one_list)(keys)


def draw_ln_gain(key, part):
    key = jax.random.fold_in(key, 2)
    values = jax.random.uniform(key, (D,), jnp.float32, 0.8, 1.25)
    return values.astype(jnp.float32)


def block_scale(own_key, extent, shards, low, largest):
    def one(axis_at, shards_of):
        heights = jax.random.uniform(jax.random.fold_in(jax.random.fold_in(own_key, 6), axis_at), (shards_of,), jnp.float32, low / len(shards), largest / len(shards))
        return jnp.repeat(jnp.exp(heights), extent[axis_at] // shards_of).reshape((-1,) + (1,) * (len(extent) - axis_at - 1))

    factor_of = one(*shards[0])
    for cut in shards[1:]:
        factor_of = factor_of * one(*cut)
    return factor_of


def noise(stream_key, extent, spread, most, cuts=(), kind=jnp.bfloat16):
    drawn = spread * jax.random.normal(stream_key, extent, jnp.float32)
    if cuts:
        drawn = drawn * block_scale(stream_key, extent, cuts, -0.22, 0.18)
    return jnp.clip(drawn, -most, most).astype(kind)


def setup_inputs(seed: int = 0) -> dict:
    key_list = jax.random.split(jax.random.key(seed), 10)
    return {
        "frames": noise(key_list[0], (RECS, FRAMES, D), 1.0, 6.0, ((0, 2), (1, 128))),
        "segments": draw_segments(jax.random.fold_in(key_list[9], 71), 0),
        "ln_gain": draw_ln_gain(jax.random.fold_in(key_list[9], 71), 0),
        "w_query": noise(key_list[3], (D, HD), D ** -0.5, 0.15625),
        "w_key": noise(key_list[4], (D, HD), D ** -0.5, 0.15625),
        "w_value": noise(key_list[5], (D, HD), D ** -0.5, 0.15625),
        "w_out": noise(key_list[6], (HD, D), HD ** -0.5, 0.25),
        "conv_gain": jnp.clip(1.0 + 0.1 * jax.random.normal(key_list[7], (D,), jnp.float32), 0.5, 1.5),
        "conv_weight": noise(key_list[8], (KSZ, D), KSZ ** -0.5, 1.0, (), jnp.float32),
    }


def normalize(values, gain):
    mean = lax.optimization_barrier(jnp.mean(values, axis=-1, keepdims=True))
    centred = values - mean
    var = lax.optimization_barrier(jnp.mean(centred * centred, axis=-1, keepdims=True))
    return centred * lax.rsqrt(var + 1e-05) * gain

def speech_mask(times, segs):
    inside = (times[:, None] >= segs[None, :, 0]) & (times[:, None] < segs[None, :, 1])
    return jnp.any(inside, axis=1)

def one_recording(x, segs, ln_gain, w_query, w_key, w_value, w_out, conv_gain, conv_weight):
    total = x.shape[0]
    block = min(512, F_DEV)
    count = total // block
    times = jnp.arange(total, dtype=jnp.int32)
    speech = speech_mask(times, segs)
    normed = normalize(x.astype(jnp.float32), ln_gain).astype(jnp.bfloat16)
    query = jnp.dot(normed, w_query, preferred_element_type=jnp.float32).astype(jnp.bfloat16)
    key = jnp.dot(normed, w_key, preferred_element_type=jnp.float32).astype(jnp.bfloat16)
    value = jnp.dot(normed, w_value, preferred_element_type=jnp.float32).astype(jnp.bfloat16)
    key_pad = jnp.concatenate([jnp.zeros((CTX, HD), jnp.bfloat16), key], axis=0)
    value_pad = jnp.concatenate([jnp.zeros((CTX, HD), jnp.bfloat16), value], axis=0)
    speech_pad = jnp.concatenate([jnp.zeros((CTX,), bool), speech], axis=0)

    def attend(index):
        first = (index * block).astype(jnp.int32)
        qs = lax.dynamic_slice_in_dim(query, first, block, 0).reshape(block, H, HS).astype(jnp.float32)
        ks = lax.dynamic_slice_in_dim(key_pad, first, block + CTX, 0).reshape(block + CTX, H, HS).astype(jnp.float32)
        vs = lax.dynamic_slice_in_dim(value_pad, first, block + CTX, 0).reshape(block + CTX, H, HS).astype(jnp.float32)
        spk = lax.dynamic_slice_in_dim(speech_pad, first, block + CTX, 0)
        tq = first + jnp.arange(block, dtype=jnp.int32)
        tk = first - CTX + jnp.arange(block + CTX, dtype=jnp.int32)
        allowed = (tk[None, :] <= tq[:, None]) & (tk[None, :] >= tq[:, None] - CTX + 1) & (tk[None, :] >= 0)
        allowed = allowed & (spk[None, :] | (tk[None, :] == tq[:, None]))
        scores = jnp.einsum('qhd,khd->hqk', qs, ks) * 0.125
        scores = jnp.where(allowed[None], scores, -jnp.inf)
        top = lax.optimization_barrier(jnp.max(scores, axis=-1, keepdims=True))
        expo = jnp.exp(scores - top)
        probs = (expo / lax.optimization_barrier(jnp.sum(expo, axis=-1, keepdims=True))).astype(jnp.bfloat16)
        out = jnp.einsum('hqk,khd->qhd', probs.astype(jnp.float32), vs)
        return out.reshape(block, HD).astype(jnp.bfloat16)
    heads_out = lax.map(attend, jnp.arange(count, dtype=jnp.int32)).reshape(total, HD)
    attn = jnp.dot(heads_out, w_out, preferred_element_type=jnp.float32)
    xf = x.astype(jnp.float32)
    hidden = jnp.where(speech[:, None], xf + attn, xf)
    conv_in = normalize(hidden, conv_gain).astype(jnp.bfloat16)
    padded = jnp.concatenate([jnp.zeros((KSZ - 1, D), jnp.bfloat16), conv_in], axis=0)
    conv = jnp.zeros((total, D), jnp.float32)
    for shift_by in range(KSZ):
        piece = padded[KSZ - 1 - shift_by:KSZ - 1 - shift_by + total].astype(jnp.float32)
        conv = conv + conv_weight[shift_by][None, :] * piece
    return jnp.where(speech[:, None], hidden + jax.nn.silu(conv), hidden).astype(jnp.bfloat16)

def reference(frames, segments, ln_gain, w_query, w_key, w_value, w_out, conv_gain, conv_weight):
    outputs = []
    for record in range(RECS):
        outputs.append(one_recording(frames[record], segments[record], ln_gain, w_query, w_key, w_value, w_out, conv_gain, conv_weight))
    return jnp.stack(outputs, axis=0)
```

```python
import jax
import jax.experimental.pallas as pl
import jax.experimental.pallas.tpu as pltpu
import jax.numpy as jnp
from jax import lax
from jax.sharding import PartitionSpec as P

H = 10
HS = 64
CTX = 256
KSZ = 31
ROWS = 256
HALO = 32
EXTRA = CTX + HALO
LANES = 128
SCALE = 0.125 * 1.4426950408889634
NEG = -1e30


def norm(values, gain):
    mean = jnp.mean(values, axis=-1, keepdims=True)
    centred = values - mean
    var = jnp.mean(centred * centred, axis=-1, keepdims=True)
    return centred * lax.rsqrt(var + 1e-05) * gain


def norm_rows(src, dst, first, count, gain_ref, step=16):
    def body(i, carry):
        rows = pl.ds(pl.multiple_of(first + i * step, 16), step)
        v = src[rows, :].astype(jnp.float32)
        dst[rows, :] = norm(v, gain_ref[...]).astype(jnp.bfloat16)
        return carry

    lax.fori_loop(0, count // step, body, 0)


def tri_masks(rows):
    i = lax.broadcasted_iota(jnp.int32, (rows, ROWS), 0)
    j = lax.broadcasted_iota(jnp.int32, (rows, ROWS), 1)
    return j <= i


def bias_row(flags, marks):
    lane = lax.broadcasted_iota(jnp.int32, (1, ROWS), 1)
    row = jnp.full((1, ROWS), NEG, jnp.float32)
    for upto, flag in reversed(marks):
        row = jnp.where(lane < upto, jnp.where(flags[flag] > 0, 0.0, NEG), row)
    return row


def attend(q_ref, q_first, k_ref, v_ref, prev_first, rows, bias, tri, heads_ref, out_first):
    cur_first = prev_first + ROWS
    lane = lax.broadcasted_iota(jnp.int32, (rows, LANES), 1)
    tri01 = jnp.where(tri, 1.0, 0.0).astype(jnp.bfloat16)
    ones = jnp.ones((ROWS, LANES), jnp.bfloat16)
    zero = jnp.zeros((rows, LANES), jnp.bfloat16)
    for pair in range(H // 2):
        cols = slice(pair * LANES, (pair + 1) * LANES)
        q = q_ref[pl.ds(q_first, rows), cols]
        kp = k_ref[pl.ds(prev_first, ROWS), cols]
        kc = k_ref[pl.ds(cur_first, ROWS), cols]
        vp = jnp.concatenate([v_ref[pl.ds(prev_first, ROWS), cols], ones], axis=1)
        vc = jnp.concatenate([v_ref[pl.ds(cur_first, ROWS), cols], ones], axis=1)
        outs = []
        for half in range(2):
            mine = (lane < HS) if half == 0 else (lane >= HS)
            qh = jnp.where(mine, q, zero)
            dims = (((1,), (1,)), ((), ()))
            sp = lax.dot_general(qh, kp, dims, preferred_element_type=jnp.float32)
            sc = lax.dot_general(qh, kc, dims, preferred_element_type=jnp.float32)
            s = jnp.where(tri, sc, sp) + bias
            top = jnp.max(s, axis=-1, keepdims=True)
            p = jnp.exp2((s - top) * SCALE).astype(jnp.bfloat16)
            pc = p * tri01
            pp = p - pc
            outs.append(
                jnp.dot(pp, vp, preferred_element_type=jnp.float32)
                + jnp.dot(pc, vc, preferred_element_type=jnp.float32)
            )
        first = lane < HS
        num = jnp.where(first, outs[0][:, :LANES], outs[1][:, :LANES])
        den = jnp.where(first, outs[0][:, LANES:], outs[1][:, LANES:])
        heads_ref[pl.ds(out_first, rows), cols] = (num / den).astype(jnp.bfloat16)


def conv_tile(cbuf, w, c, base, rows):
    acc = [None] * (rows // 8)
    for res in range(8):
        for n in range(-3, rows // 8):
            x = cbuf[c, pl.ds(base + HALO + 8 * n - res, 8), :]
            for m in range(4):
                tap = 8 * m + res
                if tap < KSZ and 0 <= n + m < rows // 8:
                    t = w[tap] * x
                    acc[n + m] = t if acc[n + m] is None else acc[n + m] + t
    return acc


def residual(x_ref, x_first, attn_ref, flags, marks, hid_ref, hid_first, cbuf, cbuf_first, gain_ref, scale=None):
    step = 16
    at = 0
    for upto, flag in marks:
        on = flags[flag] > 0

        def body(i, carry, at=at, on=on):
            here = at + i * step
            xf = x_ref[pl.ds(pl.multiple_of(x_first + here, 16), step), :].astype(jnp.float32)
            attn = attn_ref[pl.ds(pl.multiple_of(here, 16), step), :]
            hidden = jnp.where(on, xf + attn, xf)
            if hid_ref is not None:
                hid_ref[pl.ds(pl.multiple_of(hid_first + here, 16), step), :] = hidden
            cin = norm(hidden, gain_ref[...]).astype(jnp.bfloat16).astype(jnp.float32)
            if scale is not None:
                cin = cin * scale
            for c in range(10):
                cbuf[c, pl.ds(pl.multiple_of(cbuf_first + here, 16), step), :] = cin[:, c * LANES : (c + 1) * LANES]
            return carry

        lax.fori_loop(0, (upto - at) // step, body, 0)
        at = upto


def conv_rows(cbuf, w_ref, hid_ref, hid_off, flags, first, count, rows, out_ref, out_off):
    def lanes(c, carry):
        cols = pl.ds(pl.multiple_of(c * LANES, LANES), LANES)
        w = [jnp.broadcast_to(w_ref[pl.ds(j, 1), cols], (8, LANES)) for j in range(KSZ)]

        def chunk(r, inner):
            base = pl.multiple_of(first + r * rows, 32)
            acc = jnp.concatenate(conv_tile(cbuf, w, c, base, rows), axis=0)
            on = flags[3 + base // LANES] > 0
            hidden = hid_ref[pl.ds(pl.multiple_of(base + hid_off, 32), rows), cols]
            silu = acc / (1.0 + jnp.exp(-acc))
            out = jnp.where(on, hidden + silu, hidden)
            out_ref[pl.ds(pl.multiple_of(base + out_off, 32), rows), cols] = out.astype(jnp.bfloat16)
            return inner

        lax.fori_loop(0, count // rows, chunk, 0)
        return carry

    lax.fori_loop(0, 10, lanes, 0)


def kernel_a(flags, x_hbm, wq_hbm, wk_hbm, wv_hbm, wo_hbm, g1, g2, cw, out_hbm, q0, k0, v0, hid0, cin0,
             x, wqkv, wo, normed, q, k, v, heads, attn, hid, cbuf, out, sems):
    feats = H * HS
    copies = [
        pltpu.make_async_copy(x_hbm, x, sems.at[0]),
        pltpu.make_async_copy(wq_hbm, wqkv.at[:, pl.ds(0, feats)], sems.at[1]),
        pltpu.make_async_copy(wk_hbm, wqkv.at[:, pl.ds(feats, feats)], sems.at[2]),
        pltpu.make_async_copy(wv_hbm, wqkv.at[:, pl.ds(2 * feats, feats)], sems.at[3]),
        pltpu.make_async_copy(wo_hbm, wo, sems.at[4]),
    ]
    for copy in copies:
        copy.start()
    copies[0].wait()
    norm_rows(x, normed, 0, 1024, g1)
    for copy in copies[1:]:
        copy.wait()
    for b in range(4):
        rows = pl.ds(b * ROWS, ROWS)
        for part, dst in enumerate((q, k, v)):
            dst[rows, :] = jnp.dot(
                normed[rows, :], wqkv[:, part * feats : (part + 1) * feats], preferred_element_type=jnp.float32
            ).astype(jnp.bfloat16)
    q0[...] = q[0:ROWS, :]
    k0[...] = k[0:ROWS, :]
    v0[...] = v[0:ROWS, :]
    tri = tri_masks(ROWS)
    for b in range(1, 4):
        f = 3 + 2 * b
        bias = jnp.where(
            tri,
            bias_row(flags, [(128, f), (256, f + 1)]),
            bias_row(flags, [(128, f - 2), (256, f - 1)]),
        )
        attend(q, b * ROWS, k, v, (b - 1) * ROWS, ROWS, bias, tri, heads, 0)
        attn[...] = jnp.dot(heads[...], wo[...], preferred_element_type=jnp.float32)
        residual(x, b * ROWS, attn, flags, [(128, f), (256, f + 1)], hid, b * ROWS, cbuf, HALO + b * ROWS, g2)
    hid0[...] = hid[pl.ds(ROWS, HALO), :]
    cin0[...] = cbuf[:, pl.ds(HALO + ROWS, HALO), :]
    conv_rows(cbuf, cw, hid, 0, flags, EXTRA, 1024 - EXTRA, 32, out, 0)
    done = pltpu.make_async_copy(out.at[pl.ds(EXTRA, 1024 - EXTRA), :], out_hbm.at[pl.ds(EXTRA, 1024 - EXTRA), :], sems.at[5])
    done.start()
    done.wait()


def kernel_b(flags, x_hbm, tail, wq_hbm, wk_hbm, wv_hbm, wo_hbm, g1, g2, cw, q0, k0, v0, hid0, cin0, _, out_hbm,
             x, wqkv, wo, normed, q, k, v, heads, attn, hid, cbuf, out, sems):
    feats = H * HS
    copies = [
        pltpu.make_async_copy(x_hbm.at[pl.ds(0, ROWS), :], x, sems.at[0]),
        pltpu.make_async_copy(wq_hbm, wqkv.at[:, pl.ds(0, feats)], sems.at[1]),
        pltpu.make_async_copy(wk_hbm, wqkv.at[:, pl.ds(feats, feats)], sems.at[2]),
        pltpu.make_async_copy(wv_hbm, wqkv.at[:, pl.ds(2 * feats, feats)], sems.at[3]),
        pltpu.make_async_copy(wo_hbm, wo, sems.at[4]),
    ]
    for copy in copies:
        copy.start()
    norm_rows(tail, normed, 0, EXTRA, g1)
    k[pl.ds(EXTRA, ROWS), :] = k0[...]
    v[pl.ds(EXTRA, ROWS), :] = v0[...]
    q[pl.ds(HALO, ROWS), :] = q0[...]
    for copy in copies:
        copy.wait()
    q[pl.ds(0, HALO), :] = jnp.dot(
        normed[pl.ds(CTX, HALO), :], wqkv[:, :feats], preferred_element_type=jnp.float32
    ).astype(jnp.bfloat16)
    for part, dst in ((1, k), (2, v)):
        dst[pl.ds(0, EXTRA), :] = jnp.dot(
            normed[...], wqkv[:, part * feats : (part + 1) * feats], preferred_element_type=jnp.float32
        ).astype(jnp.bfloat16)
    small = tri_masks(HALO)
    bias = jnp.where(
        small, bias_row(flags, [(HALO, 2)]), bias_row(flags, [(HALO, 0), (HALO + 128, 1), (256, 2)])
    )
    attend(q, 0, k, v, 0, HALO, bias, small, heads, 0)
    tri = tri_masks(ROWS)
    bias = jnp.where(
        tri, bias_row(flags, [(128, 3), (256, 4)]), bias_row(flags, [(128, 1), (256, 2)])
    )
    attend(q, HALO, k, v, HALO, ROWS, bias, tri, heads, HALO)
    attn[...] = jnp.dot(heads[...], wo[...], preferred_element_type=jnp.float32)
    keep = jnp.where(flags[11] > 0, 1.0, 0.0)
    residual(tail, CTX, attn, flags, [(HALO, 2)], None, 0, cbuf, 0, g2, keep)
    residual(x, 0, attn.at[pl.ds(HALO, ROWS), :], flags, [(128, 3), (256, 4)], hid, 0, cbuf, HALO, g2)
    hid[pl.ds(ROWS, HALO), :] = hid0[...]
    cbuf[:, pl.ds(HALO + ROWS, HALO), :] = cin0[...]
    conv_rows(cbuf, cw, hid, 0, flags, 0, EXTRA, 32, out, 0)
    done = pltpu.make_async_copy(out, out_hbm.at[pl.ds(0, EXTRA), :], sems.at[5])
    done.start()
    done.wait()


def per_device(frames, segments, ln_gain, w_query, w_key, w_value, w_out, conv_gain, conv_weight):
    x = frames[0]
    segs = segments[0]
    count, width = x.shape
    feats = H * HS
    peers = lax.axis_size("tm")
    me = lax.axis_index("tm")
    tail = lax.ppermute(x[count - EXTRA :], "tm", [(i, i + 1) for i in range(peers - 1)])
    starts = me * count + (jnp.arange(11, dtype=jnp.int32) - 3) * LANES
    inside = (starts[:, None] >= segs[None, :, 0]) & (starts[:, None] < segs[None, :, 1])
    flags = jnp.concatenate([jnp.any(inside, axis=1).astype(jnp.int32), jnp.minimum(me, 1).reshape(1).astype(jnp.int32)])
    g1 = ln_gain.reshape(1, width)
    g2 = conv_gain.reshape(1, width)
    hbm = pl.BlockSpec(memory_space=pl.ANY)
    vmem = pl.BlockSpec(memory_space=pltpu.VMEM)
    smem = pl.BlockSpec(memory_space=pltpu.SMEM)
    bf16, f32 = jnp.bfloat16, jnp.float32
    out, q0, k0, v0, hid0, cin0 = pl.pallas_call(
        kernel_a,
        in_specs=[smem, hbm, hbm, hbm, hbm, hbm, vmem, vmem, vmem],
        out_specs=[hbm] + [vmem] * 5,
        out_shape=[
            jax.ShapeDtypeStruct((count, width), bf16),
            jax.ShapeDtypeStruct((ROWS, feats), bf16),
            jax.ShapeDtypeStruct((ROWS, feats), bf16),
            jax.ShapeDtypeStruct((ROWS, feats), bf16),
            jax.ShapeDtypeStruct((HALO, width), f32),
            jax.ShapeDtypeStruct((10, HALO, LANES), f32),
        ],
        scratch_shapes=[
            pltpu.VMEM((count, width), bf16),
            pltpu.VMEM((width, 3 * feats), bf16),
            pltpu.VMEM((feats, width), bf16),
            pltpu.VMEM((count, width), bf16),
            pltpu.VMEM((count, feats), bf16),
            pltpu.VMEM((count, feats), bf16),
            pltpu.VMEM((count, feats), bf16),
            pltpu.VMEM((ROWS, feats), bf16),
            pltpu.VMEM((ROWS, width), f32),
            pltpu.VMEM((count, width), f32),
            pltpu.VMEM((10, HALO + count, LANES), f32),
            pltpu.VMEM((count, width), bf16),
            pltpu.SemaphoreType.DMA((6,)),
        ],
        compiler_params=pltpu.CompilerParams(vmem_limit_bytes=56 << 20),
        cost_estimate=pl.CostEstimate(flops=12_000_000_000, bytes_accessed=11_000_000, transcendentals=4_000_000),
        name="own_rows",
    )(flags, x, w_query, w_key, w_value, w_out, g1, g2, conv_weight)
    out = pl.pallas_call(
        kernel_b,
        in_specs=[smem, hbm, vmem, hbm, hbm, hbm, hbm] + [vmem] * 8 + [hbm],
        out_specs=hbm,
        out_shape=jax.ShapeDtypeStruct((count, width), bf16),
        input_output_aliases={15: 0},
        scratch_shapes=[
            pltpu.VMEM((ROWS, width), bf16),
            pltpu.VMEM((width, 3 * feats), bf16),
            pltpu.VMEM((feats, width), bf16),
            pltpu.VMEM((EXTRA, width), bf16),
            pltpu.VMEM((EXTRA, feats), bf16),
            pltpu.VMEM((EXTRA + ROWS, feats), bf16),
            pltpu.VMEM((EXTRA + ROWS, feats), bf16),
            pltpu.VMEM((EXTRA, feats), bf16),
            pltpu.VMEM((EXTRA, width), f32),
            pltpu.VMEM((EXTRA, width), f32),
            pltpu.VMEM((10, HALO + EXTRA, LANES), f32),
            pltpu.VMEM((EXTRA, width), bf16),
            pltpu.SemaphoreType.DMA((6,)),
        ],
        compiler_params=pltpu.CompilerParams(vmem_limit_bytes=56 << 20),
        cost_estimate=pl.CostEstimate(flops=4_000_000_000, bytes_accessed=9_000_000, transcendentals=1_000_000),
        name="first_rows",
    )(flags, x, tail, w_query, w_key, w_value, w_out, g1, g2, conv_weight, q0, k0, v0, hid0, cin0, out)
    return out[None]


def solution(mesh):
    in_specs = (P("rec", "tm", None), P("rec", None, None), P(), P(), P(), P(), P(), P(), P())
    out_specs = P("rec", "tm", None)
    return jax.shard_map(
        per_device, mesh=mesh, in_specs=in_specs, out_specs=out_specs, check_vma=False
    )
```

```python
import jax
import jax.experimental.pallas as pl
import jax.experimental.pallas.tpu as pltpu
import jax.numpy as jnp
from jax import lax
from jax.sharding import PartitionSpec as P

H = 10
HS = 64
CTX = 256
KSZ = 31
ROWS = 256
HALO = 32
EXTRA = CTX + HALO
SEGS = 256
SPLIT = 480
LANES = 128
SCALE = 0.125 * 1.4426950408889634
NEG = -1e30


def lane_sum(v):
    total = v[:, :LANES]
    for t in range(1, v.shape[1] // LANES):
        total = total + v[:, t * LANES : (t + 1) * LANES]
    return jnp.sum(total, axis=-1, keepdims=True) * (1.0 / v.shape[1])


def norm_staged(load, store, count, gain, step=16):
    means, scales = [], []
    for r in range(0, count, step):
        means.append(lane_sum(load(r, True)))
    for mean, r in zip(means, range(0, count, step)):
        centred = load(r, False) - mean
        scales.append(lax.rsqrt(lane_sum(centred * centred) + 1e-05))
    for mean, scale, r in zip(means, scales, range(0, count, step)):
        store(r, (load(r, False) - mean) * scale * gain)


def norm_rows(src, dst, first, count, gain, step=16):
    def load(r, _):
        return src[pl.ds(pl.multiple_of(first + r, 16), step), :].astype(jnp.float32)

    def store(r, value):
        dst[pl.ds(pl.multiple_of(first + r, 16), step), :] = value.astype(jnp.bfloat16)

    norm_staged(load, store, count, gain, step)


def tri_masks(rows):
    i = lax.broadcasted_iota(jnp.int32, (rows, ROWS), 0)
    j = lax.broadcasted_iota(jnp.int32, (rows, ROWS), 1)
    return j <= i


def bias_row(flags, marks):
    lane = lax.broadcasted_iota(jnp.int32, (1, ROWS), 1)
    row = jnp.full((1, ROWS), NEG, jnp.float32)
    for upto, flag in reversed(marks):
        row = jnp.where(lane < upto, jnp.where(flags[flag] > 0, 0.0, NEG), row)
    return row


def attend(q_ref, q_first, k_ref, v_ref, prev_first, rows, bias, tri, heads_ref, out_first):
    cur_first = prev_first + ROWS
    lane = lax.broadcasted_iota(jnp.int32, (rows, LANES), 1)
    tri01 = jnp.where(tri, 1.0, 0.0).astype(jnp.bfloat16)
    ones = jnp.ones((ROWS, LANES), jnp.bfloat16)
    zero = jnp.zeros((rows, LANES), jnp.bfloat16)
    for pair in range(H // 2):
        cols = slice(pair * LANES, (pair + 1) * LANES)
        q = q_ref[pl.ds(q_first, rows), cols]
        kp = k_ref[pl.ds(prev_first, ROWS), cols]
        kc = k_ref[pl.ds(cur_first, ROWS), cols]
        vp = jnp.concatenate([v_ref[pl.ds(prev_first, ROWS), cols], ones], axis=1)
        vc = jnp.concatenate([v_ref[pl.ds(cur_first, ROWS), cols], ones], axis=1)
        outs = []
        for half in range(2):
            mine = (lane < HS) if half == 0 else (lane >= HS)
            qh = jnp.where(mine, q, zero)
            dims = (((1,), (1,)), ((), ()))
            sp = lax.dot_general(qh, kp, dims, preferred_element_type=jnp.float32)
            sc = lax.dot_general(qh, kc, dims, preferred_element_type=jnp.float32)
            s = jnp.where(tri, sc, sp) + bias
            top = jnp.max(s, axis=-1, keepdims=True)
            p = jnp.exp2((s - top) * SCALE).astype(jnp.bfloat16)
            pc = p * tri01
            pp = p - pc
            outs.append(
                jnp.dot(pp, vp, preferred_element_type=jnp.float32)
                + jnp.dot(pc, vc, preferred_element_type=jnp.float32)
            )
        first = lane < HS
        num = jnp.where(first, outs[0][:, :LANES], outs[1][:, :LANES])
        den = jnp.where(first, outs[0][:, LANES:], outs[1][:, LANES:])
        heads_ref[pl.ds(out_first, rows), cols] = (num / den).astype(jnp.bfloat16)


def fir_weights(w_ref, cols):
    def add(a, b):
        return a if b is None else a + b

    w = [w_ref[pl.ds(j, 1), cols] for j in range(KSZ)] + [None]
    even, odd = w[0::2], w[1::2]
    sets = []
    for h in (even, odd, [add(a, b) for a, b in zip(even, odd)]):
        first, second = h[0::2], h[1::2]
        sets += [first, second, [add(a, b) for a, b in zip(first, second)]]
    return [[None if t is None else jnp.broadcast_to(t, (8, LANES)) for t in h] for h in sets]


def conv_seg(cbuf, w_ref, c, cols, base, units, comb, part, ybuf):
    seg = 4 * units
    weights = fir_weights(w_ref, cols)
    for u in range(-8, units):
        x = [cbuf[c, pl.ds(base + HALO + 4 * u + p, 8, stride=seg), :] for p in range(4)]
        low, high = x[0] + x[1], x[2] + x[3]
        for f, t in enumerate((x[0], x[2], x[0] + x[2], x[1], x[3], x[1] + x[3], low, high, low + high)):
            comb[f, u + 8] = t
    for f, h in enumerate(weights):
        lo = 0 if f in (0, 2, 6, 8) else -1
        xs = {u: comb[f, u + 8] for u in range(lo - 7, units)}
        for u in range(lo, units):
            acc = None
            for m in range(8):
                if h[m] is not None:
                    t = h[m] * xs[u - m]
                    acc = t if acc is None else acc + t
            part[f, u + 1] = acc
    b1, b4, b7 = part[1, 0], part[4, 0], part[7, 0]
    before = part[5, 0] - (part[3, 0] + b4)
    for u in range(units):
        b = [part[f, u + 1] for f in range(9)]
        a1e, a1o = b[0] + b1, b[2] - (b[0] + b[1])
        a2e, a2o = b[3] + b4, b[5] - (b[3] + b[4])
        a3e, a3o = b[6] + b7, b[8] - (b[6] + b[7])
        y = (a1e + before, a3e - (a1e + a2e), a1o + a2e, a3o - (a1o + a2o))
        b1, b4, b7, before = b[1], b[4], b[7], a2o
        for p in range(4):
            ybuf[pl.ds(4 * u + p, 8, stride=seg), :] = y[p]


def residual(x_ref, x_first, attn_ref, flags, marks, hid_ref, hid_first, cbuf, cbuf_first, gain, scale=None):
    def load(r, first):
        if not first:
            return hid_ref[pl.ds(hid_first + r, 16), :]
        on = [flags[flag] for upto, flag in reversed(marks) if r < upto][-1] > 0
        xf = x_ref[pl.ds(x_first + r, 16), :].astype(jnp.float32)
        hidden = jnp.where(on, xf + attn_ref[pl.ds(r, 16), :], xf)
        hid_ref[pl.ds(hid_first + r, 16), :] = hidden
        return hidden

    def store(r, value):
        value = value.astype(jnp.bfloat16).astype(jnp.float32)
        if scale is not None:
            value = value * scale
        for c in range(10):
            cbuf[c, pl.ds(cbuf_first + r, 16), :] = value[:, c * LANES : (c + 1) * LANES]

    norm_staged(load, store, marks[-1][0], gain)


def conv_rows(cbuf, w_ref, hid_ref, flags, first, units, comb, part, ybuf, out_ref, out_hbm, sems):
    count = 32 * units

    def lanes(c, carry):
        cols = pl.ds(pl.multiple_of(c * LANES, LANES), LANES)
        conv_seg(cbuf, w_ref, c, cols, first, units, comb, part, ybuf)
        for r in range(0, count, 32):
            on = flags[3 + (first + r) // LANES] > 0
            half = ybuf[pl.ds(r, 32), :] * 0.5
            hidden = hid_ref[pl.ds(first + r, 32), cols]
            out = jnp.where(on, hidden + (half + half * jnp.tanh(half)), hidden)
            out_ref[pl.ds(r, 32), cols] = out.astype(jnp.bfloat16)
        send(c).start()
        return carry

    def send(c):
        cols = pl.ds(pl.multiple_of(c * LANES, LANES), LANES)
        return pltpu.make_async_copy(
            out_ref.at[:, cols], out_hbm.at[pl.ds(first, count), cols], sems.at[c]
        )

    def finish(c, carry):
        send(c).wait()
        return carry

    lax.fori_loop(0, 10, lanes, 0)
    lax.fori_loop(0, 10, finish, 0)


def block_flags(segs, base):
    times = [base + (i - 3) * LANES for i in range(11)]
    lows = [jnp.int32(0)] * 11
    step = SEGS // 2
    while step:
        lows = [jnp.where(segs[2 * (lo + step)] <= t, lo + step, lo) for lo, t in zip(lows, times)]
        step //= 2
    return [
        ((t >= 0) & (segs[2 * lo] <= t) & (t < segs[2 * lo + 1])).astype(jnp.int32) for lo, t in zip(lows, times)
    ]


def kernel_a(segs, place, x_hbm, wq_hbm, wk_hbm, wv_hbm, wo_hbm, g1, g2, cw, out_hbm, q0, k0, v0, hid0, cin0, flags0,
             x, wqkv, wo, normed, q, k, v, heads, attn, hid, cbuf, out, comb, part, ybuf, sems, out_sems):
    feats = H * HS
    copies = [
        pltpu.make_async_copy(x_hbm, x, sems.at[0]),
        pltpu.make_async_copy(wq_hbm, wqkv.at[:, pl.ds(0, feats)], sems.at[1]),
        pltpu.make_async_copy(wk_hbm, wqkv.at[:, pl.ds(feats, feats)], sems.at[2]),
        pltpu.make_async_copy(wv_hbm, wqkv.at[:, pl.ds(2 * feats, feats)], sems.at[3]),
        pltpu.make_async_copy(wo_hbm, wo, sems.at[4]),
    ]
    for copy in copies:
        copy.start()
    flags = block_flags(segs, place[0])
    for i in range(11):
        flags0[i] = flags[i]
    flags0[11] = jnp.minimum(place[0], 1)
    gain1 = g1[...].reshape(1, -1)
    gain2 = g2[...].reshape(1, -1)
    copies[0].wait()
    for b in range(4):
        norm_rows(x, normed, b * ROWS, ROWS, gain1)
    for copy in copies[1:]:
        copy.wait()
    for b in range(4):
        rows = pl.ds(b * ROWS, ROWS)
        for part_at, dst in enumerate((q, k, v)):
            dst[rows, :] = jnp.dot(
                normed[rows, :], wqkv[:, part_at * feats : (part_at + 1) * feats], preferred_element_type=jnp.float32
            ).astype(jnp.bfloat16)
    first = [pltpu.make_async_copy(src.at[pl.ds(0, ROWS), :], dst, sems.at[i]) for i, (src, dst) in enumerate(((q, q0), (k, k0), (v, v0)))]
    for copy in first:
        copy.start()
    tri = tri_masks(ROWS)
    for b in range(1, 4):
        f = 3 + 2 * b
        bias = jnp.where(
            tri,
            bias_row(flags, [(128, f), (256, f + 1)]),
            bias_row(flags, [(128, f - 2), (256, f - 1)]),
        )
        attend(q, b * ROWS, k, v, (b - 1) * ROWS, ROWS, bias, tri, heads, 0)
        attn[...] = jnp.dot(heads[...], wo[...], preferred_element_type=jnp.float32)
        residual(x, b * ROWS, attn, flags, [(128, f), (256, f + 1)], hid, b * ROWS, cbuf, HALO + b * ROWS, gain2)
    rest = [
        pltpu.make_async_copy(hid.at[pl.ds(ROWS, SPLIT - ROWS), :], hid0, sems.at[3]),
        pltpu.make_async_copy(cbuf.at[:, pl.ds(HALO + ROWS, SPLIT - ROWS), :], cin0, sems.at[4]),
    ]
    for copy in rest:
        copy.start()
    conv_rows(cbuf, cw, hid, flags, SPLIT, (1024 - SPLIT) // 32, comb, part, ybuf, out, out_hbm, out_sems)
    for copy in first + rest:
        copy.wait()


def kernel_b(flags, x_hbm, tail_hbm, wq_hbm, wk_hbm, wv_hbm, wo_hbm, g1, g2, cw, q0, k0, v0, hid0, cin0, _, out_hbm,
             tail, x, wqkv, wo, normed, q, k, v, heads, attn, hid, halo_hid, cbuf, out, comb, part, ybuf, sems, out_sems):
    feats = H * HS
    copies = [
        pltpu.make_async_copy(tail_hbm, tail, sems.at[0]),
        pltpu.make_async_copy(wq_hbm, wqkv.at[:, pl.ds(0, feats)], sems.at[1]),
        pltpu.make_async_copy(wk_hbm, wqkv.at[:, pl.ds(feats, feats)], sems.at[2]),
        pltpu.make_async_copy(wv_hbm, wqkv.at[:, pl.ds(2 * feats, feats)], sems.at[3]),
        pltpu.make_async_copy(q0, q.at[pl.ds(HALO, ROWS), :], sems.at[4]),
        pltpu.make_async_copy(k0, k.at[pl.ds(EXTRA, ROWS), :], sems.at[5]),
        pltpu.make_async_copy(v0, v.at[pl.ds(EXTRA, ROWS), :], sems.at[6]),
        pltpu.make_async_copy(wo_hbm, wo, sems.at[7]),
        pltpu.make_async_copy(x_hbm.at[pl.ds(0, ROWS), :], x, sems.at[8]),
        pltpu.make_async_copy(hid0, hid.at[pl.ds(ROWS, SPLIT - ROWS), :], sems.at[9]),
        pltpu.make_async_copy(cin0, cbuf.at[:, pl.ds(HALO + ROWS, SPLIT - ROWS), :], sems.at[10]),
    ]
    for copy in copies:
        copy.start()
    gain1 = g1[...].reshape(1, -1)
    gain2 = g2[...].reshape(1, -1)
    copies[0].wait()
    norm_rows(tail, normed, 0, EXTRA, gain1)
    for copy in copies[1:7]:
        copy.wait()
    q[pl.ds(0, HALO), :] = jnp.dot(
        normed[pl.ds(CTX, HALO), :], wqkv[:, :feats], preferred_element_type=jnp.float32
    ).astype(jnp.bfloat16)
    for part_at, dst in ((1, k), (2, v)):
        dst[pl.ds(0, EXTRA), :] = jnp.dot(
            normed[...], wqkv[:, part_at * feats : (part_at + 1) * feats], preferred_element_type=jnp.float32
        ).astype(jnp.bfloat16)
    small = tri_masks(HALO)
    bias = jnp.where(
        small, bias_row(flags, [(HALO, 2)]), bias_row(flags, [(HALO, 0), (HALO + 128, 1), (256, 2)])
    )
    attend(q, 0, k, v, 0, HALO, bias, small, heads, 0)
    tri = tri_masks(ROWS)
    bias = jnp.where(
        tri, bias_row(flags, [(128, 3), (256, 4)]), bias_row(flags, [(128, 1), (256, 2)])
    )
    attend(q, HALO, k, v, HALO, ROWS, bias, tri, heads, HALO)
    for copy in copies[7:]:
        copy.wait()
    attn[...] = jnp.dot(heads[...], wo[...], preferred_element_type=jnp.float32)
    keep = jnp.where(flags[11] > 0, 1.0, 0.0)
    residual(tail, CTX, attn, flags, [(HALO, 2)], halo_hid, 0, cbuf, 0, gain2, keep)
    residual(x, 0, attn.at[pl.ds(HALO, ROWS), :], flags, [(128, 3), (256, 4)], hid, 0, cbuf, HALO, gain2)
    conv_rows(cbuf, cw, hid, flags, 0, SPLIT // 32, comb, part, ybuf, out, out_hbm, out_sems)


def per_device(frames, segments, ln_gain, w_query, w_key, w_value, w_out, conv_gain, conv_weight):
    x = frames[0]
    count, width = x.shape
    feats = H * HS
    peers = lax.axis_size("tm")
    me = lax.axis_index("tm")
    tail = lax.ppermute(x[count - EXTRA :], "tm", [(i, i + 1) for i in range(peers - 1)])
    place = (me * count).reshape(1).astype(jnp.int32)
    segs = segments.reshape(2 * SEGS)
    hbm = pl.BlockSpec(memory_space=pl.ANY)
    vmem = pl.BlockSpec(memory_space=pltpu.VMEM)
    smem = pl.BlockSpec(memory_space=pltpu.SMEM)
    bf16, f32 = jnp.bfloat16, jnp.float32
    late = count - SPLIT
    out, q0, k0, v0, hid0, cin0, flags = pl.pallas_call(
        kernel_a,
        in_specs=[smem, smem, hbm, hbm, hbm, hbm, hbm, vmem, vmem, vmem],
        out_specs=[hbm] * 6 + [smem],
        out_shape=[
            jax.ShapeDtypeStruct((count, width), bf16),
            jax.ShapeDtypeStruct((ROWS, feats), bf16),
            jax.ShapeDtypeStruct((ROWS, feats), bf16),
            jax.ShapeDtypeStruct((ROWS, feats), bf16),
            jax.ShapeDtypeStruct((SPLIT - ROWS, width), f32),
            jax.ShapeDtypeStruct((10, SPLIT - ROWS, LANES), f32),
            jax.ShapeDtypeStruct((12,), jnp.int32),
        ],
        scratch_shapes=[
            pltpu.VMEM((count, width), bf16),
            pltpu.VMEM((width, 3 * feats), bf16),
            pltpu.VMEM((feats, width), bf16),
            pltpu.VMEM((count, width), bf16),
            pltpu.VMEM((count, feats), bf16),
            pltpu.VMEM((count, feats), bf16),
            pltpu.VMEM((count, feats), bf16),
            pltpu.VMEM((ROWS, feats), bf16),
            pltpu.VMEM((ROWS, width), f32),
            pltpu.VMEM((count, width), f32),
            pltpu.VMEM((10, HALO + count, LANES), f32),
            pltpu.VMEM((late, width), bf16),
            pltpu.VMEM((9, late // 32 + 8, 8, LANES), f32),
            pltpu.VMEM((9, late // 32 + 1, 8, LANES), f32),
            pltpu.VMEM((late, LANES), f32),
            pltpu.SemaphoreType.DMA((5,)),
            pltpu.SemaphoreType.DMA((10,)),
        ],
        compiler_params=pltpu.CompilerParams(vmem_limit_bytes=56 << 20),
        cost_estimate=pl.CostEstimate(flops=12_000_000_000, bytes_accessed=11_000_000, transcendentals=4_000_000),
        name="own_rows",
    )(segs, place, x, w_query, w_key, w_value, w_out, ln_gain, conv_gain, conv_weight)
    out = pl.pallas_call(
        kernel_b,
        in_specs=[smem] + [hbm] * 6 + [vmem] * 3 + [hbm] * 6,
        out_specs=hbm,
        out_shape=jax.ShapeDtypeStruct((count, width), bf16),
        input_output_aliases={15: 0},
        scratch_shapes=[
            pltpu.VMEM((EXTRA, width), bf16),
            pltpu.VMEM((ROWS, width), bf16),
            pltpu.VMEM((width, 3 * feats), bf16),
            pltpu.VMEM((feats, width), bf16),
            pltpu.VMEM((EXTRA, width), bf16),
            pltpu.VMEM((EXTRA, feats), bf16),
            pltpu.VMEM((EXTRA + ROWS, feats), bf16),
            pltpu.VMEM((EXTRA + ROWS, feats), bf16),
            pltpu.VMEM((EXTRA, feats), bf16),
            pltpu.VMEM((EXTRA, width), f32),
            pltpu.VMEM((SPLIT, width), f32),
            pltpu.VMEM((HALO, width), f32),
            pltpu.VMEM((10, HALO + SPLIT, LANES), f32),
            pltpu.VMEM((SPLIT, width), bf16),
            pltpu.VMEM((9, SPLIT // 32 + 8, 8, LANES), f32),
            pltpu.VMEM((9, SPLIT // 32 + 1, 8, LANES), f32),
            pltpu.VMEM((SPLIT, LANES), f32),
            pltpu.SemaphoreType.DMA((11,)),
            pltpu.SemaphoreType.DMA((10,)),
        ],
        compiler_params=pltpu.CompilerParams(vmem_limit_bytes=56 << 20),
        cost_estimate=pl.CostEstimate(flops=4_000_000_000, bytes_accessed=9_000_000, transcendentals=1_000_000),
        name="first_rows",
    )(flags, x, tail, w_query, w_key, w_value, w_out, ln_gain, conv_gain, conv_weight, q0, k0, v0, hid0, cin0, out)
    return out[None]


def solution(mesh):
    in_specs = (P("rec", "tm", None), P("rec", None, None), P(), P(), P(), P(), P(), P(), P())
    out_specs = P("rec", "tm", None)
    return jax.shard_map(
        per_device, mesh=mesh, in_specs=in_specs, out_specs=out_specs, check_vma=False
    )
```

```python
import jax
import jax.experimental.pallas as pl
import jax.experimental.pallas.tpu as pltpu
import jax.numpy as jnp
from jax import lax
from jax.sharding import PartitionSpec as P

H = 10
HS = 64
CTX = 256
KSZ = 31
ROWS = 256
HALO = 32
EXTRA = CTX + HALO
SEGS = 256
SPLIT = 480
LANES = 128
SCALE = 0.125 * 1.4426950408889634
NEG = -1e30


def lane_sum(v):
    total = v[:, :LANES]
    for t in range(1, v.shape[1] // LANES):
        total = total + v[:, t * LANES : (t + 1) * LANES]
    return jnp.sum(total, axis=-1, keepdims=True) * (1.0 / v.shape[1])


def norm_staged(load, store, count, gain, step=16):
    means, scales = [], []
    for r in range(0, count, step):
        means.append(lane_sum(load(r, True)))
    for mean, r in zip(means, range(0, count, step)):
        centred = load(r, False) - mean
        scales.append(lax.rsqrt(lane_sum(centred * centred) + 1e-05))
    for mean, scale, r in zip(means, scales, range(0, count, step)):
        store(r, (load(r, False) - mean) * scale * gain)


def norm_rows(src, dst, first, count, gain, step=16):
    def load(r, _):
        return src[pl.ds(pl.multiple_of(first + r, 16), step), :].astype(jnp.float32)

    def store(r, value):
        dst[pl.ds(pl.multiple_of(first + r, 16), step), :] = value.astype(jnp.bfloat16)

    norm_staged(load, store, count, gain, step)


def tri_masks(rows):
    i = lax.broadcasted_iota(jnp.int32, (rows, ROWS), 0)
    j = lax.broadcasted_iota(jnp.int32, (rows, ROWS), 1)
    return j <= i


def bias_row(flags, marks):
    lane = lax.broadcasted_iota(jnp.int32, (1, ROWS), 1)
    row = jnp.full((1, ROWS), NEG, jnp.float32)
    for upto, flag in reversed(marks):
        row = jnp.where(lane < upto, jnp.where(flags[flag] > 0, 0.0, NEG), row)
    return row


def attend(q_ref, q_first, k_ref, v_ref, prev_first, rows, bias, tri, heads_ref, out_first):
    cur_first = prev_first + ROWS
    lane = lax.broadcasted_iota(jnp.int32, (rows, LANES), 1)
    tri01 = jnp.where(tri, 1.0, 0.0).astype(jnp.bfloat16)
    ones = jnp.ones((ROWS, LANES), jnp.bfloat16)
    zero = jnp.zeros((rows, LANES), jnp.bfloat16)
    for pair in range(H // 2):
        cols = slice(pair * LANES, (pair + 1) * LANES)
        q = q_ref[pl.ds(q_first, rows), cols]
        kp = k_ref[pl.ds(prev_first, ROWS), cols]
        kc = k_ref[pl.ds(cur_first, ROWS), cols]
        vp = jnp.concatenate([v_ref[pl.ds(prev_first, ROWS), cols], ones], axis=1)
        vc = jnp.concatenate([v_ref[pl.ds(cur_first, ROWS), cols], ones], axis=1)
        outs = []
        for half in range(2):
            mine = (lane < HS) if half == 0 else (lane >= HS)
            qh = jnp.where(mine, q, zero)
            dims = (((1,), (1,)), ((), ()))
            sp = lax.dot_general(qh, kp, dims, preferred_element_type=jnp.float32)
            sc = lax.dot_general(qh, kc, dims, preferred_element_type=jnp.float32)
            s = jnp.where(tri, sc, sp) + bias
            top = jnp.max(s, axis=-1, keepdims=True)
            p = jnp.exp2((s - top) * SCALE).astype(jnp.bfloat16)
            pc = p * tri01
            pp = p - pc
            outs.append(
                jnp.dot(pp, vp, preferred_element_type=jnp.float32)
                + jnp.dot(pc, vc, preferred_element_type=jnp.float32)
            )
        first = lane < HS
        num = jnp.where(first, outs[0][:, :LANES], outs[1][:, :LANES])
        den = jnp.where(first, outs[0][:, LANES:], outs[1][:, LANES:])
        heads_ref[pl.ds(out_first, rows), cols] = (num / den).astype(jnp.bfloat16)


def fir_weights(w_ref, cols):
    def add(a, b):
        return a if b is None else a + b

    w = [w_ref[pl.ds(j, 1), cols] for j in range(KSZ)] + [None]
    even, odd = w[0::2], w[1::2]
    sets = []
    for h in (even, odd, [add(a, b) for a, b in zip(even, odd)]):
        first, second = h[0::2], h[1::2]
        sets += [first, second, [add(a, b) for a, b in zip(first, second)]]
    return [[None if t is None else jnp.broadcast_to(t, (8, LANES)) for t in h] for h in sets]


def conv_seg(cbuf, w_ref, c, cols, base, units, comb, part, ybuf):
    seg = 4 * units
    weights = fir_weights(w_ref, cols)
    for u in range(-8, units):
        x = [cbuf[c, pl.ds(base + HALO + 4 * u + p, 8, stride=seg), :] for p in range(4)]
        low, high = x[0] + x[1], x[2] + x[3]
        for f, t in enumerate((x[0], x[2], x[0] + x[2], x[1], x[3], x[1] + x[3], low, high, low + high)):
            comb[f, u + 8] = t
    for f, h in enumerate(weights):
        lo = 0 if f in (0, 2, 6, 8) else -1
        xs = {u: comb[f, u + 8] for u in range(lo - 7, units)}
        for u in range(lo, units):
            acc = None
            for m in range(8):
                if h[m] is not None:
                    t = h[m] * xs[u - m]
                    acc = t if acc is None else acc + t
            part[f, u + 1] = acc
    b1, b4, b7 = part[1, 0], part[4, 0], part[7, 0]
    before = part[5, 0] - (part[3, 0] + b4)
    for u in range(units):
        b = [part[f, u + 1] for f in range(9)]
        a1e, a1o = b[0] + b1, b[2] - (b[0] + b[1])
        a2e, a2o = b[3] + b4, b[5] - (b[3] + b[4])
        a3e, a3o = b[6] + b7, b[8] - (b[6] + b[7])
        y = (a1e + before, a3e - (a1e + a2e), a1o + a2e, a3o - (a1o + a2o))
        b1, b4, b7, before = b[1], b[4], b[7], a2o
        for p in range(4):
            ybuf[pl.ds(4 * u + p, 8, stride=seg), :] = y[p]


def residual(x_ref, x_first, attn_ref, flags, marks, hid_ref, hid_first, cbuf, cbuf_first, gain, scale=None):
    def load(r, first):
        if not first:
            return hid_ref[pl.ds(hid_first + r, 16), :]
        on = [flags[flag] for upto, flag in reversed(marks) if r < upto][-1] > 0
        xf = x_ref[pl.ds(x_first + r, 16), :].astype(jnp.float32)
        hidden = jnp.where(on, xf + attn_ref[pl.ds(r, 16), :], xf)
        hid_ref[pl.ds(hid_first + r, 16), :] = hidden
        return hidden

    def store(r, value):
        value = value.astype(jnp.bfloat16).astype(jnp.float32)
        if scale is not None:
            value = value * scale
        for c in range(10):
            cbuf[c, pl.ds(cbuf_first + r, 16), :] = value[:, c * LANES : (c + 1) * LANES]

    norm_staged(load, store, marks[-1][0], gain)


def conv_rows(cbuf, w_ref, hid_ref, flags, first, units, comb, part, ybuf, out_ref, out_hbm, sems):
    count = 32 * units

    def lanes(c, carry):
        cols = pl.ds(pl.multiple_of(c * LANES, LANES), LANES)
        conv_seg(cbuf, w_ref, c, cols, first, units, comb, part, ybuf)
        for r in range(0, count, 32):
            on = flags[3 + (first + r) // LANES] > 0
            half = ybuf[pl.ds(r, 32), :] * 0.5
            hidden = hid_ref[pl.ds(first + r, 32), cols]
            out = jnp.where(on, hidden + (half + half * jnp.tanh(half)), hidden)
            out_ref[pl.ds(r, 32), cols] = out.astype(jnp.bfloat16)
        send(c).start()
        return carry

    def send(c):
        cols = pl.ds(pl.multiple_of(c * LANES, LANES), LANES)
        return pltpu.make_async_copy(
            out_ref.at[:, cols], out_hbm.at[pl.ds(first, count), cols], sems.at[c]
        )

    def finish(c, carry):
        send(c).wait()
        return carry

    lax.fori_loop(0, 10, lanes, 0)
    lax.fori_loop(0, 10, finish, 0)


def block_flags(segs, base):
    times = [base + (i - 3) * LANES for i in range(11)]
    lows = [jnp.int32(0)] * 11
    step = SEGS // 2
    while step:
        lows = [jnp.where(segs[0, lo + step] <= t, lo + step, lo) for lo, t in zip(lows, times)]
        step //= 2
    return [
        ((t >= 0) & (segs[0, lo] <= t) & (t < segs[1, lo])).astype(jnp.int32) for lo, t in zip(lows, times)
    ]


def kernel_a(segs, place, x_hbm, wq_hbm, wk_hbm, wv_hbm, wo_hbm, g1, g2, cw, out_hbm, q0, kv0, hid0, cin0, flags0,
             x, wqkv, wo, normed, qkv, heads, attn, hid, cbuf, out, comb, part, ybuf, sems, out_sems):
    feats = H * HS
    q, k, v = (qkv.at[:, pl.ds(i * feats, feats)] for i in range(3))
    copies = [
        pltpu.make_async_copy(x_hbm.at[pl.ds(b * ROWS, ROWS), :], x.at[pl.ds(b * ROWS, ROWS), :], sems.at[b])
        for b in range(4)
    ] + [
        pltpu.make_async_copy(wq_hbm, wqkv.at[:, pl.ds(0, feats)], sems.at[4]),
        pltpu.make_async_copy(wk_hbm, wqkv.at[:, pl.ds(feats, feats)], sems.at[5]),
        pltpu.make_async_copy(wv_hbm, wqkv.at[:, pl.ds(2 * feats, feats)], sems.at[6]),
        pltpu.make_async_copy(wo_hbm, wo, sems.at[7]),
    ]
    for i in (0, 4, 1, 2, 3, 5, 6, 7):
        copies[i].start()
    flags = block_flags(segs, place[0])
    for i in range(11):
        flags0[i] = flags[i]
    flags0[11] = jnp.minimum(place[0], 1)
    gain1 = g1[...].reshape(1, -1)
    gain2 = g2[...].reshape(1, -1)
    def project(b, lo, hi):
        rows = pl.ds(b * ROWS, ROWS)
        qkv[rows, lo:hi] = jnp.dot(
            normed[rows, :], wqkv[:, lo:hi], preferred_element_type=jnp.float32
        ).astype(jnp.bfloat16)

    for b in range(4):
        copies[b].wait()
        norm_rows(x, normed, b * ROWS, ROWS, gain1)
        if b == 0:
            copies[4].wait()
        project(b, 0, 512)
    for i, lo, hi in ((5, 512, 2 * feats), (6, 2 * feats, 3 * feats)):
        copies[i].wait()
        for b in range(4):
            project(b, lo, hi)
    copies[7].wait()
    first = [
        pltpu.make_async_copy(qkv.at[pl.ds(0, ROWS), pl.ds(0, feats)], q0, sems.at[0]),
        pltpu.make_async_copy(qkv.at[pl.ds(0, ROWS), pl.ds(feats, 2 * feats)], kv0, sems.at[1]),
    ]
    for copy in first:
        copy.start()
    tri = tri_masks(ROWS)
    for b in range(1, 4):
        f = 3 + 2 * b
        bias = jnp.where(
            tri,
            bias_row(flags, [(128, f), (256, f + 1)]),
            bias_row(flags, [(128, f - 2), (256, f - 1)]),
        )
        attend(q, b * ROWS, k, v, (b - 1) * ROWS, ROWS, bias, tri, heads, (b - 1) * ROWS)
    attn[...] = jnp.dot(heads[...], wo[...], preferred_element_type=jnp.float32)
    for b in range(1, 4):
        f = 3 + 2 * b
        residual(x, b * ROWS, attn.at[pl.ds((b - 1) * ROWS, ROWS), :], flags, [(128, f), (256, f + 1)], hid, b * ROWS, cbuf, HALO + b * ROWS, gain2)
    rest = [
        pltpu.make_async_copy(hid.at[pl.ds(ROWS, SPLIT - ROWS), :], hid0, sems.at[3]),
        pltpu.make_async_copy(cbuf.at[:, pl.ds(HALO + ROWS, SPLIT - ROWS), :], cin0, sems.at[4]),
    ]
    for copy in rest:
        copy.start()
    conv_rows(cbuf, cw, hid, flags, SPLIT, (1024 - SPLIT) // 32, comb, part, ybuf, out, out_hbm, out_sems)
    for copy in first + rest:
        copy.wait()


def kernel_b(flags, x_hbm, tail_hbm, wq_hbm, wk_hbm, wv_hbm, wo_hbm, g1, g2, cw, q0, kv0, hid0, cin0, _, out_hbm,
             tail, x, wqkv, wo, normed, q, kv, heads, attn, hid, halo_hid, cbuf, out, comb, part, ybuf, sems, out_sems):
    feats = H * HS
    k, v = (kv.at[:, pl.ds(i * feats, feats)] for i in range(2))
    copies = [
        pltpu.make_async_copy(tail_hbm, tail, sems.at[0]),
        pltpu.make_async_copy(wk_hbm, wqkv.at[:, pl.ds(feats, feats)], sems.at[1]),
        pltpu.make_async_copy(wv_hbm, wqkv.at[:, pl.ds(2 * feats, feats)], sems.at[2]),
        pltpu.make_async_copy(wq_hbm, wqkv.at[:, pl.ds(0, feats)], sems.at[3]),
        pltpu.make_async_copy(q0, q.at[pl.ds(HALO, ROWS), :], sems.at[4]),
        pltpu.make_async_copy(kv0, kv.at[pl.ds(EXTRA, ROWS), :], sems.at[5]),
        pltpu.make_async_copy(wo_hbm, wo, sems.at[6]),
        pltpu.make_async_copy(x_hbm.at[pl.ds(0, ROWS), :], x, sems.at[7]),
        pltpu.make_async_copy(hid0, hid.at[pl.ds(ROWS, SPLIT - ROWS), :], sems.at[8]),
        pltpu.make_async_copy(cin0, cbuf.at[:, pl.ds(HALO + ROWS, SPLIT - ROWS), :], sems.at[9]),
    ]
    for copy in copies:
        copy.start()
    gain1 = g1[...].reshape(1, -1)
    gain2 = g2[...].reshape(1, -1)
    copies[0].wait()
    norm_rows(tail, normed, 0, EXTRA, gain1)
    for i, lo, hi in ((1, 0, 512), (2, 512, 2 * feats)):
        copies[i].wait()
        kv[pl.ds(0, EXTRA), lo:hi] = jnp.dot(
            normed[...], wqkv[:, feats + lo : feats + hi], preferred_element_type=jnp.float32
        ).astype(jnp.bfloat16)
    copies[3].wait()
    q[pl.ds(0, HALO), :] = jnp.dot(
        normed[pl.ds(CTX, HALO), :], wqkv[:, :feats], preferred_element_type=jnp.float32
    ).astype(jnp.bfloat16)
    copies[4].wait()
    copies[5].wait()
    small = tri_masks(HALO)
    bias = jnp.where(
        small, bias_row(flags, [(HALO, 2)]), bias_row(flags, [(HALO, 0), (HALO + 128, 1), (256, 2)])
    )
    attend(q, 0, k, v, 0, HALO, bias, small, heads, 0)
    tri = tri_masks(ROWS)
    bias = jnp.where(
        tri, bias_row(flags, [(128, 3), (256, 4)]), bias_row(flags, [(128, 1), (256, 2)])
    )
    attend(q, HALO, k, v, HALO, ROWS, bias, tri, heads, HALO)
    for copy in copies[6:]:
        copy.wait()
    attn[...] = jnp.dot(heads[...], wo[...], preferred_element_type=jnp.float32)
    keep = jnp.where(flags[11] > 0, 1.0, 0.0)
    residual(tail, CTX, attn, flags, [(HALO, 2)], halo_hid, 0, cbuf, 0, gain2, keep)
    residual(x, 0, attn.at[pl.ds(HALO, ROWS), :], flags, [(128, 3), (256, 4)], hid, 0, cbuf, HALO, gain2)
    conv_rows(cbuf, cw, hid, flags, 0, SPLIT // 32, comb, part, ybuf, out, out_hbm, out_sems)


def per_device(frames, segments, ln_gain, w_query, w_key, w_value, w_out, conv_gain, conv_weight):
    x = frames[0]
    count, width = x.shape
    feats = H * HS
    peers = lax.axis_size("tm")
    me = lax.axis_index("tm")
    tail = lax.ppermute(x[count - EXTRA :], "tm", [(i, i + 1) for i in range(peers - 1)])
    place = (me * count).reshape(1).astype(jnp.int32)
    segs = segments[0].T
    hbm = pl.BlockSpec(memory_space=pl.ANY)
    vmem = pl.BlockSpec(memory_space=pltpu.VMEM)
    smem = pl.BlockSpec(memory_space=pltpu.SMEM)
    bf16, f32 = jnp.bfloat16, jnp.float32
    late = count - SPLIT
    out, q0, kv0, hid0, cin0, flags = pl.pallas_call(
        kernel_a,
        in_specs=[smem, smem, hbm, hbm, hbm, hbm, hbm, vmem, vmem, vmem],
        out_specs=[hbm] * 5 + [smem],
        out_shape=[
            jax.ShapeDtypeStruct((count, width), bf16),
            jax.ShapeDtypeStruct((ROWS, feats), bf16),
            jax.ShapeDtypeStruct((ROWS, 2 * feats), bf16),
            jax.ShapeDtypeStruct((SPLIT - ROWS, width), f32),
            jax.ShapeDtypeStruct((10, SPLIT - ROWS, LANES), f32),
            jax.ShapeDtypeStruct((12,), jnp.int32),
        ],
        scratch_shapes=[
            pltpu.VMEM((count, width), bf16),
            pltpu.VMEM((width, 3 * feats), bf16),
            pltpu.VMEM((feats, width), bf16),
            pltpu.VMEM((count, width), bf16),
            pltpu.VMEM((count, 3 * feats), bf16),
            pltpu.VMEM((count - ROWS, feats), bf16),
            pltpu.VMEM((count - ROWS, width), f32),
            pltpu.VMEM((count, width), f32),
            pltpu.VMEM((10, HALO + count, LANES), f32),
            pltpu.VMEM((late, width), bf16),
            pltpu.VMEM((9, late // 32 + 8, 8, LANES), f32),
            pltpu.VMEM((9, late // 32 + 1, 8, LANES), f32),
            pltpu.VMEM((late, LANES), f32),
            pltpu.SemaphoreType.DMA((8,)),
            pltpu.SemaphoreType.DMA((10,)),
        ],
        compiler_params=pltpu.CompilerParams(vmem_limit_bytes=56 << 20),
        cost_estimate=pl.CostEstimate(flops=12_000_000_000, bytes_accessed=11_000_000, transcendentals=4_000_000),
        name="own_rows",
    )(segs, place, x, w_query, w_key, w_value, w_out, ln_gain, conv_gain, conv_weight)
    out = pl.pallas_call(
        kernel_b,
        in_specs=[smem, hbm, pl.BlockSpec(memory_space=pltpu.HBM)] + [hbm] * 4 + [vmem] * 3 + [hbm] * 5,
        out_specs=hbm,
        out_shape=jax.ShapeDtypeStruct((count, width), bf16),
        input_output_aliases={14: 0},
        scratch_shapes=[
            pltpu.VMEM((EXTRA, width), bf16),
            pltpu.VMEM((ROWS, width), bf16),
            pltpu.VMEM((width, 3 * feats), bf16),
            pltpu.VMEM((feats, width), bf16),
            pltpu.VMEM((EXTRA, width), bf16),
            pltpu.VMEM((EXTRA, feats), bf16),
            pltpu.VMEM((EXTRA + ROWS, 2 * feats), bf16),
            pltpu.VMEM((EXTRA, feats), bf16),
            pltpu.VMEM((EXTRA, width), f32),
            pltpu.VMEM((SPLIT, width), f32),
            pltpu.VMEM((HALO, width), f32),
            pltpu.VMEM((10, HALO + SPLIT, LANES), f32),
            pltpu.VMEM((SPLIT, width), bf16),
            pltpu.VMEM((9, SPLIT // 32 + 8, 8, LANES), f32),
            pltpu.VMEM((9, SPLIT // 32 + 1, 8, LANES), f32),
            pltpu.VMEM((SPLIT, LANES), f32),
            pltpu.SemaphoreType.DMA((10,)),
            pltpu.SemaphoreType.DMA((10,)),
        ],
        compiler_params=pltpu.CompilerParams(vmem_limit_bytes=56 << 20),
        cost_estimate=pl.CostEstimate(flops=4_000_000_000, bytes_accessed=9_000_000, transcendentals=1_000_000),
        name="first_rows",
    )(flags, x, tail, w_query, w_key, w_value, w_out, ln_gain, conv_gain, conv_weight, q0, kv0, hid0, cin0, out)
    return out[None]


def solution(mesh):
    in_specs = (P("rec", "tm", None), P("rec", None, None), P(), P(), P(), P(), P(), P(), P())
    out_specs = P("rec", "tm", None)
    return jax.shard_map(
        per_device, mesh=mesh, in_specs=in_specs, out_specs=out_specs, check_vma=False
    )
```

```python
import jax
import jax.experimental.pallas as pl
import jax.experimental.pallas.tpu as pltpu
import jax.numpy as jnp
from jax import lax
from jax.sharding import PartitionSpec as P

H = 10
HS = 64
CTX = 256
KSZ = 31
ROWS = 256
HALO = 32
EXTRA = CTX + HALO
SEGS = 256
SPLIT = 480
LANES = 128
SCALE = 0.125 * 1.4426950408889634
NEG = -1e30


def lane_sum(v):
    total = v[:, :LANES]
    for t in range(1, v.shape[1] // LANES):
        total = total + v[:, t * LANES : (t + 1) * LANES]
    return jnp.sum(total, axis=-1, keepdims=True) * (1.0 / v.shape[1])


def norm_staged(load, store, count, gain, step=16):
    means, scales = [], []
    for r in range(0, count, step):
        means.append(lane_sum(load(r, True)))
    for mean, r in zip(means, range(0, count, step)):
        centred = load(r, False) - mean
        scales.append(lax.rsqrt(lane_sum(centred * centred) + 1e-05))
    for mean, scale, r in zip(means, scales, range(0, count, step)):
        store(r, (load(r, False) - mean) * scale * gain)


def norm_rows(src, dst, first, count, gain, step=16):
    def load(r, _):
        return src[pl.ds(pl.multiple_of(first + r, 16), step), :].astype(jnp.float32)

    def store(r, value):
        dst[pl.ds(pl.multiple_of(first + r, 16), step), :] = value.astype(jnp.bfloat16)

    norm_staged(load, store, count, gain, step)


def tri_masks(rows):
    i = lax.broadcasted_iota(jnp.int32, (rows, ROWS), 0)
    j = lax.broadcasted_iota(jnp.int32, (rows, ROWS), 1)
    return j <= i


def bias_row(flags, marks):
    lane = lax.broadcasted_iota(jnp.int32, (1, ROWS), 1)
    row = jnp.full((1, ROWS), NEG, jnp.float32)
    for upto, flag in reversed(marks):
        row = jnp.where(lane < upto, jnp.where(flags[flag] > 0, 0.0, NEG), row)
    return row


def attend(q_ref, q_first, k_ref, v_ref, prev_first, rows, bias, tri, heads_ref, out_first):
    cur_first = prev_first + ROWS
    stack = rows < ROWS
    lane = lax.broadcasted_iota(jnp.int32, (rows, LANES), 1)
    if stack:
        tri = jnp.concatenate([tri, tri], axis=0)
        bias = jnp.concatenate([bias, bias], axis=0)
    tri01 = jnp.where(tri, 1.0, 0.0).astype(jnp.bfloat16)
    ones = jnp.ones((ROWS, LANES), jnp.bfloat16)
    zero = jnp.zeros((rows, LANES), jnp.bfloat16)
    dims = (((1,), (1,)), ((), ()))
    for pair in range(H // 2):
        cols = slice(pair * LANES, (pair + 1) * LANES)
        q = q_ref[pl.ds(q_first, rows), cols]
        kp = k_ref[pl.ds(prev_first, ROWS), cols]
        kc = k_ref[pl.ds(cur_first, ROWS), cols]
        vp = jnp.concatenate([v_ref[pl.ds(prev_first, ROWS), cols], ones], axis=1)
        vc = jnp.concatenate([v_ref[pl.ds(cur_first, ROWS), cols], ones], axis=1)
        halves = [jnp.where(lane < HS, q, zero), jnp.where(lane >= HS, q, zero)]
        if stack:
            halves = [jnp.concatenate(halves, axis=0)]
        outs = []
        for qh in halves:
            sp = lax.dot_general(qh, kp, dims, preferred_element_type=jnp.float32)
            sc = lax.dot_general(qh, kc, dims, preferred_element_type=jnp.float32)
            s = jnp.where(tri, sc, sp) + bias
            top = jnp.max(s, axis=-1, keepdims=True)
            p = jnp.exp2((s - top) * SCALE).astype(jnp.bfloat16)
            pc = p * tri01
            pp = p - pc
            outs.append(
                jnp.dot(pp, vp, preferred_element_type=jnp.float32)
                + jnp.dot(pc, vc, preferred_element_type=jnp.float32)
            )
        if stack:
            outs = [outs[0][:rows], outs[0][rows:]]
        first = lane < HS
        num = jnp.where(first, outs[0][:, :LANES], outs[1][:, :LANES])
        den = jnp.where(first, outs[0][:, LANES:], outs[1][:, LANES:])
        heads_ref[pl.ds(out_first, rows), cols] = (num / den).astype(jnp.bfloat16)


def fill_weights(w_ref, table):
    def add(a, b):
        return a if b is None else a + b

    w = [w_ref[pl.ds(j, 1), :] * 0.5 for j in range(KSZ)] + [None]
    even, odd = w[0::2], w[1::2]
    sets = []
    for h in (even, odd, [add(a, b) for a, b in zip(even, odd)]):
        first, second = h[0::2], h[1::2]
        sets += [first, second, [add(a, b) for a, b in zip(first, second)]]
    for f, h in enumerate(sets):
        for m, t in enumerate(h):
            table[pl.ds(8 * f + m, 1), :] = jnp.zeros_like(w[0]) if t is None else t


def conv_seg(cbuf, w_ref, c, cols, base, units, comb, part, ybuf):
    seg = 4 * units
    zero_tap = (4, 7)
    for u in range(-8, units):
        x = [cbuf[c, pl.ds(base + HALO + 4 * u + p, 8, stride=seg), :] for p in range(4)]
        low, high = x[0] + x[1], x[2] + x[3]
        for f, t in enumerate((x[0], x[2], x[0] + x[2], x[1], x[3], x[1] + x[3], low, high, low + high)):
            comb[f, u + 8] = t
    for f in range(9):
        h = [
            None if (f, m) == zero_tap else jnp.broadcast_to(w_ref[pl.ds(8 * f + m, 1), cols], (8, LANES))
            for m in range(8)
        ]
        lo = 0 if f in (0, 2, 6, 8) else -1
        xs = {u: comb[f, u + 8] for u in range(lo - 7, units)}
        for u in range(lo, units):
            acc = None
            for m in range(8):
                if h[m] is not None:
                    t = h[m] * xs[u - m]
                    acc = t if acc is None else acc + t
            part[f, u + 1] = acc
    b1, b4, b7 = part[1, 0], part[4, 0], part[7, 0]
    before = part[5, 0] - (part[3, 0] + b4)
    for u in range(units):
        b = [part[f, u + 1] for f in range(9)]
        a1e, a1o = b[0] + b1, b[2] - (b[0] + b[1])
        a2e, a2o = b[3] + b4, b[5] - (b[3] + b[4])
        a3e, a3o = b[6] + b7, b[8] - (b[6] + b[7])
        y = (a1e + before, a3e - (a1e + a2e), a1o + a2e, a3o - (a1o + a2o))
        b1, b4, b7, before = b[1], b[4], b[7], a2o
        for p in range(4):
            ybuf[pl.ds(4 * u + p, 8, stride=seg), :] = y[p]


def residual(x_ref, x_first, attn_ref, flags, marks, hid_ref, hid_first, cbuf, cbuf_first, gain, scale=None):
    def load(r, first):
        if not first:
            return hid_ref[pl.ds(hid_first + r, 16), :]
        on = [flags[flag] for upto, flag in reversed(marks) if r < upto][-1] > 0
        xf = x_ref[pl.ds(x_first + r, 16), :].astype(jnp.float32)
        hidden = jnp.where(on, xf + attn_ref[pl.ds(r, 16), :], xf)
        hid_ref[pl.ds(hid_first + r, 16), :] = hidden
        return hidden

    def store(r, value):
        value = value.astype(jnp.bfloat16).astype(jnp.float32)
        if scale is not None:
            value = value * scale
        for c in range(10):
            cbuf[c, pl.ds(cbuf_first + r, 16), :] = value[:, c * LANES : (c + 1) * LANES]

    norm_staged(load, store, marks[-1][0], gain)


def conv_rows(cbuf, w_ref, hid_ref, flags, first, units, comb, part, ybuf, out_ref, out_hbm, sems):
    count = 32 * units

    def lanes(c, carry):
        cols = pl.ds(pl.multiple_of(c * LANES, LANES), LANES)
        conv_seg(cbuf, w_ref, c, cols, first, units, comb, part, ybuf)
        for r in range(0, count, 32):
            on = flags[3 + (first + r) // LANES] > 0
            half = ybuf[pl.ds(r, 32), :]
            hidden = hid_ref[pl.ds(first + r, 32), cols]
            out = jnp.where(on, hidden + (half + half * jnp.tanh(half)), hidden)
            out_ref[pl.ds(r, 32), cols] = out.astype(jnp.bfloat16)
        send(c).start()
        return carry

    def send(c):
        cols = pl.ds(pl.multiple_of(c * LANES, LANES), LANES)
        return pltpu.make_async_copy(
            out_ref.at[:, cols], out_hbm.at[pl.ds(first, count), cols], sems.at[c]
        )

    def finish(c, carry):
        send(c).wait()
        return carry

    lax.fori_loop(0, 10, lanes, 0)
    lax.fori_loop(0, 10, finish, 0)


def block_flags(segs, base):
    times = [base + (i - 3) * LANES for i in range(11)]
    lows = [jnp.int32(0)] * 11
    step = SEGS // 2
    while step:
        lows = [jnp.where(segs[0, lo + step] <= t, lo + step, lo) for lo, t in zip(lows, times)]
        step //= 2
    return [
        ((t >= 0) & (segs[0, lo] <= t) & (t < segs[1, lo])).astype(jnp.int32) for lo, t in zip(lows, times)
    ]


def kernel_a(segs, place, x_hbm, wq_hbm, wk_hbm, wv_hbm, wo_hbm, g1, g2, cw, out_hbm, q0, kv0, hid0, cin0, flags0,
             x, wqkv, wo, normed, qkv, heads, attn, hid, cbuf, out, comb, part, ybuf, sems, out_sems, table):
    feats = H * HS
    q, k, v = (qkv.at[:, pl.ds(i * feats, feats)] for i in range(3))
    copies = [
        pltpu.make_async_copy(x_hbm.at[pl.ds(b * ROWS, ROWS), :], x.at[pl.ds(b * ROWS, ROWS), :], sems.at[b])
        for b in range(4)
    ] + [
        pltpu.make_async_copy(wq_hbm, wqkv.at[:, pl.ds(0, feats)], sems.at[4]),
        pltpu.make_async_copy(wk_hbm, wqkv.at[:, pl.ds(feats, feats)], sems.at[5]),
        pltpu.make_async_copy(wv_hbm, wqkv.at[:, pl.ds(2 * feats, feats)], sems.at[6]),
        pltpu.make_async_copy(wo_hbm, wo, sems.at[7]),
    ]
    for i in (0, 4, 1, 2, 3, 5, 6, 7):
        copies[i].start()
    flags = block_flags(segs, place[0])
    for i in range(11):
        flags0[i] = flags[i]
    flags0[11] = jnp.minimum(place[0], 1)
    fill_weights(cw, table)
    gain1 = g1[...].reshape(1, -1)
    gain2 = g2[...].reshape(1, -1)
    def project(b, lo, hi):
        rows = pl.ds(b * ROWS, ROWS)
        qkv[rows, lo:hi] = jnp.dot(
            normed[rows, :], wqkv[:, lo:hi], preferred_element_type=jnp.float32
        ).astype(jnp.bfloat16)

    for b in range(4):
        copies[b].wait()
        norm_rows(x, normed, b * ROWS, ROWS, gain1)
        if b == 0:
            copies[4].wait()
        project(b, 0, 512)
    for i, lo, hi in ((5, 512, 2 * feats), (6, 2 * feats, 3 * feats)):
        copies[i].wait()
        for b in range(4):
            project(b, lo, hi)
    copies[7].wait()
    first = [
        pltpu.make_async_copy(qkv.at[pl.ds(0, ROWS), pl.ds(0, feats)], q0, sems.at[0]),
        pltpu.make_async_copy(qkv.at[pl.ds(0, ROWS), pl.ds(feats, 2 * feats)], kv0, sems.at[1]),
    ]
    for copy in first:
        copy.start()
    tri = tri_masks(ROWS)
    for b in range(1, 4):
        f = 3 + 2 * b
        bias = jnp.where(
            tri,
            bias_row(flags, [(128, f), (256, f + 1)]),
            bias_row(flags, [(128, f - 2), (256, f - 1)]),
        )
        attend(q, b * ROWS, k, v, (b - 1) * ROWS, ROWS, bias, tri, heads, (b - 1) * ROWS)
    attn[...] = jnp.dot(heads[...], wo[...], preferred_element_type=jnp.float32)
    for b in range(1, 4):
        f = 3 + 2 * b
        residual(x, b * ROWS, attn.at[pl.ds((b - 1) * ROWS, ROWS), :], flags, [(128, f), (256, f + 1)], hid, b * ROWS, cbuf, HALO + b * ROWS, gain2)
    rest = [
        pltpu.make_async_copy(hid.at[pl.ds(ROWS, SPLIT - ROWS), :], hid0, sems.at[3]),
        pltpu.make_async_copy(cbuf.at[:, pl.ds(HALO + ROWS, SPLIT - ROWS), :], cin0, sems.at[4]),
    ]
    for copy in rest:
        copy.start()
    conv_rows(cbuf, table, hid, flags, SPLIT, (1024 - SPLIT) // 32, comb, part, ybuf, out, out_hbm, out_sems)
    for copy in first + rest:
        copy.wait()


def kernel_b(flags, x_hbm, tail_hbm, wq_hbm, wk_hbm, wv_hbm, wo_hbm, g1, g2, cw, q0, kv0, hid0, cin0, _, out_hbm,
             tail, x, wqkv, wo, normed, q, kv, heads, attn, hid, halo_hid, cbuf, out, comb, part, ybuf, sems, out_sems, table):
    feats = H * HS
    k, v = (kv.at[:, pl.ds(i * feats, feats)] for i in range(2))
    copies = [
        pltpu.make_async_copy(tail_hbm, tail, sems.at[0]),
        pltpu.make_async_copy(wk_hbm, wqkv.at[:, pl.ds(feats, feats)], sems.at[1]),
        pltpu.make_async_copy(wv_hbm, wqkv.at[:, pl.ds(2 * feats, feats)], sems.at[2]),
        pltpu.make_async_copy(wq_hbm, wqkv.at[:, pl.ds(0, feats)], sems.at[3]),
        pltpu.make_async_copy(q0, q.at[pl.ds(HALO, ROWS), :], sems.at[4]),
        pltpu.make_async_copy(kv0, kv.at[pl.ds(EXTRA, ROWS), :], sems.at[5]),
        pltpu.make_async_copy(wo_hbm, wo, sems.at[6]),
        pltpu.make_async_copy(x_hbm.at[pl.ds(0, ROWS), :], x, sems.at[7]),
        pltpu.make_async_copy(hid0, hid.at[pl.ds(ROWS, SPLIT - ROWS), :], sems.at[8]),
        pltpu.make_async_copy(cin0, cbuf.at[:, pl.ds(HALO + ROWS, SPLIT - ROWS), :], sems.at[9]),
    ]
    for copy in copies:
        copy.start()
    fill_weights(cw, table)
    gain1 = g1[...].reshape(1, -1)
    gain2 = g2[...].reshape(1, -1)
    copies[0].wait()
    norm_rows(tail, normed, 0, EXTRA, gain1)
    for i, lo, hi in ((1, 0, 512), (2, 512, 2 * feats)):
        copies[i].wait()
        kv[pl.ds(0, EXTRA), lo:hi] = jnp.dot(
            normed[...], wqkv[:, feats + lo : feats + hi], preferred_element_type=jnp.float32
        ).astype(jnp.bfloat16)
    copies[3].wait()
    q[pl.ds(0, HALO), :] = jnp.dot(
        normed[pl.ds(CTX, HALO), :], wqkv[:, :feats], preferred_element_type=jnp.float32
    ).astype(jnp.bfloat16)
    copies[4].wait()
    copies[5].wait()
    small = tri_masks(HALO)
    bias = jnp.where(
        small, bias_row(flags, [(HALO, 2)]), bias_row(flags, [(HALO, 0), (HALO + 128, 1), (256, 2)])
    )
    attend(q, 0, k, v, 0, HALO, bias, small, heads, 0)
    tri = tri_masks(ROWS)
    bias = jnp.where(
        tri, bias_row(flags, [(128, 3), (256, 4)]), bias_row(flags, [(128, 1), (256, 2)])
    )
    attend(q, HALO, k, v, HALO, ROWS, bias, tri, heads, HALO)
    for copy in copies[6:]:
        copy.wait()
    attn[...] = jnp.dot(heads[...], wo[...], preferred_element_type=jnp.float32)
    keep = jnp.where(flags[11] > 0, 1.0, 0.0)
    residual(tail, CTX, attn, flags, [(HALO, 2)], halo_hid, 0, cbuf, 0, gain2, keep)
    residual(x, 0, attn.at[pl.ds(HALO, ROWS), :], flags, [(128, 3), (256, 4)], hid, 0, cbuf, HALO, gain2)
    conv_rows(cbuf, table, hid, flags, 0, SPLIT // 32, comb, part, ybuf, out, out_hbm, out_sems)


def per_device(frames, segments, ln_gain, w_query, w_key, w_value, w_out, conv_gain, conv_weight):
    x = frames[0]
    count, width = x.shape
    feats = H * HS
    peers = lax.axis_size("tm")
    me = lax.axis_index("tm")
    tail = lax.ppermute(x[count - EXTRA :], "tm", [(i, i + 1) for i in range(peers - 1)])
    place = (me * count).reshape(1).astype(jnp.int32)
    segs = segments[0].T
    hbm = pl.BlockSpec(memory_space=pl.ANY)
    vmem = pl.BlockSpec(memory_space=pltpu.VMEM)
    smem = pl.BlockSpec(memory_space=pltpu.SMEM)
    bf16, f32 = jnp.bfloat16, jnp.float32
    late = count - SPLIT
    out, q0, kv0, hid0, cin0, flags = pl.pallas_call(
        kernel_a,
        in_specs=[smem, smem, hbm, hbm, hbm, hbm, hbm, vmem, vmem, vmem],
        out_specs=[hbm] * 5 + [smem],
        out_shape=[
            jax.ShapeDtypeStruct((count, width), bf16),
            jax.ShapeDtypeStruct((ROWS, feats), bf16),
            jax.ShapeDtypeStruct((ROWS, 2 * feats), bf16),
            jax.ShapeDtypeStruct((SPLIT - ROWS, width), f32),
            jax.ShapeDtypeStruct((10, SPLIT - ROWS, LANES), f32),
            jax.ShapeDtypeStruct((12,), jnp.int32),
        ],
        scratch_shapes=[
            pltpu.VMEM((count, width), bf16),
            pltpu.VMEM((width, 3 * feats), bf16),
            pltpu.VMEM((feats, width), bf16),
            pltpu.VMEM((count, width), bf16),
            pltpu.VMEM((count, 3 * feats), bf16),
            pltpu.VMEM((count - ROWS, feats), bf16),
            pltpu.VMEM((count - ROWS, width), f32),
            pltpu.VMEM((count, width), f32),
            pltpu.VMEM((10, HALO + count, LANES), f32),
            pltpu.VMEM((late, width), bf16),
            pltpu.VMEM((9, late // 32 + 8, 8, LANES), f32),
            pltpu.VMEM((9, late // 32 + 1, 8, LANES), f32),
            pltpu.VMEM((late, LANES), f32),
            pltpu.SemaphoreType.DMA((8,)),
            pltpu.SemaphoreType.DMA((10,)),
            pltpu.VMEM((72, width), f32),
        ],
        compiler_params=pltpu.CompilerParams(vmem_limit_bytes=63 << 20),
        cost_estimate=pl.CostEstimate(flops=12_000_000_000, bytes_accessed=11_000_000, transcendentals=4_000_000),
        name="own_rows",
    )(segs, place, x, w_query, w_key, w_value, w_out, ln_gain, conv_gain, conv_weight)
    out = pl.pallas_call(
        kernel_b,
        in_specs=[smem, hbm, pl.BlockSpec(memory_space=pltpu.HBM)] + [hbm] * 4 + [vmem] * 3 + [hbm] * 5,
        out_specs=hbm,
        out_shape=jax.ShapeDtypeStruct((count, width), bf16),
        input_output_aliases={14: 0},
        scratch_shapes=[
            pltpu.VMEM((EXTRA, width), bf16),
            pltpu.VMEM((ROWS, width), bf16),
            pltpu.VMEM((width, 3 * feats), bf16),
            pltpu.VMEM((feats, width), bf16),
            pltpu.VMEM((EXTRA, width), bf16),
            pltpu.VMEM((EXTRA, feats), bf16),
            pltpu.VMEM((EXTRA + ROWS, 2 * feats), bf16),
            pltpu.VMEM((EXTRA, feats), bf16),
            pltpu.VMEM((EXTRA, width), f32),
            pltpu.VMEM((SPLIT, width), f32),
            pltpu.VMEM((HALO, width), f32),
            pltpu.VMEM((10, HALO + SPLIT, LANES), f32),
            pltpu.VMEM((SPLIT, width), bf16),
            pltpu.VMEM((9, SPLIT // 32 + 8, 8, LANES), f32),
            pltpu.VMEM((9, SPLIT // 32 + 1, 8, LANES), f32),
            pltpu.VMEM((SPLIT, LANES), f32),
            pltpu.SemaphoreType.DMA((10,)),
            pltpu.SemaphoreType.DMA((10,)),
            pltpu.VMEM((72, width), f32),
        ],
        compiler_params=pltpu.CompilerParams(vmem_limit_bytes=63 << 20),
        cost_estimate=pl.CostEstimate(flops=4_000_000_000, bytes_accessed=9_000_000, transcendentals=1_000_000),
        name="first_rows",
    )(flags, x, tail, w_query, w_key, w_value, w_out, ln_gain, conv_gain, conv_weight, q0, kv0, hid0, cin0, out)
    return out[None]


def solution(mesh):
    in_specs = (P("rec", "tm", None), P("rec", None, None), P(), P(), P(), P(), P(), P(), P())
    out_specs = P("rec", "tm", None)
    return jax.shard_map(
        per_device, mesh=mesh, in_specs=in_specs, out_specs=out_specs, check_vma=False
    )
```

```python
import jax
import jax.experimental.pallas as pl
import jax.experimental.pallas.tpu as pltpu
import jax.numpy as jnp
from jax import lax
from jax.sharding import PartitionSpec as P

H = 10
HS = 64
CTX = 256
KSZ = 31
ROWS = 256
HALO = 32
EXTRA = CTX + HALO
SEGS = 256
SPLIT = 480
LANES = 128
SCALE = 0.125 * 1.4426950408889634
NEG = -1e30


def lane_sum(v):
    total = v[:, :LANES]
    for t in range(1, v.shape[1] // LANES):
        total = total + v[:, t * LANES : (t + 1) * LANES]
    return jnp.sum(total, axis=-1, keepdims=True) * (1.0 / v.shape[1])


def norm_staged(load, store, count, gain, step=16):
    means, scales = [], []
    for r in range(0, count, step):
        means.append(lane_sum(load(r, True)))
    for mean, r in zip(means, range(0, count, step)):
        centred = load(r, False) - mean
        scales.append(lax.rsqrt(lane_sum(centred * centred) + 1e-05))
    for mean, scale, r in zip(means, scales, range(0, count, step)):
        store(r, (load(r, False) - mean) * scale * gain)


def norm_rows(src, dst, first, count, gain, step=16):
    def load(r, _):
        return src[pl.ds(pl.multiple_of(first + r, 16), step), :].astype(jnp.float32)

    def store(r, value):
        dst[pl.ds(pl.multiple_of(first + r, 16), step), :] = value.astype(jnp.bfloat16)

    norm_staged(load, store, count, gain, step)


def tri_masks(rows):
    i = lax.broadcasted_iota(jnp.int32, (rows, ROWS), 0)
    j = lax.broadcasted_iota(jnp.int32, (rows, ROWS), 1)
    return j <= i


def bias_row(flags, marks):
    lane = lax.broadcasted_iota(jnp.int32, (1, ROWS), 1)
    row = jnp.full((1, ROWS), NEG, jnp.float32)
    for upto, flag in reversed(marks):
        row = jnp.where(lane < upto, jnp.where(flags[flag] > 0, 0.0, NEG), row)
    return row


def attend(q_ref, q_first, k_ref, v_ref, prev_first, rows, bias, tri, heads_ref, out_first):
    cur_first = prev_first + ROWS
    stack = rows < ROWS
    lane = lax.broadcasted_iota(jnp.int32, (rows, LANES), 1)
    if stack:
        tri = jnp.concatenate([tri, tri], axis=0)
        bias = jnp.concatenate([bias, bias], axis=0)
    tri01 = jnp.where(tri, 1.0, 0.0).astype(jnp.bfloat16)
    ones = jnp.ones((ROWS, LANES), jnp.bfloat16)
    zero = jnp.zeros((rows, LANES), jnp.bfloat16)
    dims = (((1,), (1,)), ((), ()))
    for pair in range(H // 2):
        cols = slice(pair * LANES, (pair + 1) * LANES)
        q = q_ref[pl.ds(q_first, rows), cols]
        kp = k_ref[pl.ds(prev_first, ROWS), cols]
        kc = k_ref[pl.ds(cur_first, ROWS), cols]
        vp = jnp.concatenate([v_ref[pl.ds(prev_first, ROWS), cols], ones], axis=1)
        vc = jnp.concatenate([v_ref[pl.ds(cur_first, ROWS), cols], ones], axis=1)
        halves = [jnp.where(lane < HS, q, zero), jnp.where(lane >= HS, q, zero)]
        if stack:
            halves = [jnp.concatenate(halves, axis=0)]
        outs = []
        for qh in halves:
            sp = lax.dot_general(qh, kp, dims, preferred_element_type=jnp.float32)
            sc = lax.dot_general(qh, kc, dims, preferred_element_type=jnp.float32)
            s = jnp.where(tri, sc, sp) + bias
            top = jnp.max(s, axis=-1, keepdims=True)
            p = jnp.exp2((s - top) * SCALE).astype(jnp.bfloat16)
            pc = p * tri01
            pp = p - pc
            outs.append(
                jnp.dot(pp, vp, preferred_element_type=jnp.float32)
                + jnp.dot(pc, vc, preferred_element_type=jnp.float32)
            )
        if stack:
            outs = [outs[0][:rows], outs[0][rows:]]
        first = lane < HS
        num = jnp.where(first, outs[0][:, :LANES], outs[1][:, :LANES])
        den = jnp.where(first, outs[0][:, LANES:], outs[1][:, LANES:])
        heads_ref[pl.ds(out_first, rows), cols] = (num / den).astype(jnp.bfloat16)


def fill_weights(w_ref, table):
    def add(a, b):
        return a if b is None else a + b

    w = [w_ref[pl.ds(j, 1), :] * 0.5 for j in range(KSZ)] + [None]
    even, odd = w[0::2], w[1::2]
    sets = []
    for h in (even, odd, [add(a, b) for a, b in zip(even, odd)]):
        first, second = h[0::2], h[1::2]
        sets += [first, second, [add(a, b) for a, b in zip(first, second)]]
    for f, h in enumerate(sets):
        for m, t in enumerate(h):
            table[pl.ds(8 * f + m, 1), :] = jnp.zeros_like(w[0]) if t is None else t


def conv_seg(cbuf, w_ref, c, cols, base, units, comb, part, ybuf):
    seg = 4 * units
    zero_tap = (4, 7)
    for u in range(-8, units):
        x = [cbuf[c, pl.ds(base + HALO + 4 * u + p, 8, stride=seg), :] for p in range(4)]
        low, high = x[0] + x[1], x[2] + x[3]
        for f, t in enumerate((x[0], x[2], x[0] + x[2], x[1], x[3], x[1] + x[3], low, high, low + high)):
            comb[f, u + 8] = t
    for f in range(9):
        h = [
            None if (f, m) == zero_tap else jnp.broadcast_to(w_ref[pl.ds(8 * f + m, 1), cols], (8, LANES))
            for m in range(8)
        ]
        lo = 0 if f in (0, 2, 6, 8) else -1
        xs = {u: comb[f, u + 8] for u in range(lo - 7, units)}
        for u in range(lo, units):
            acc = None
            for m in range(8):
                if h[m] is not None:
                    t = h[m] * xs[u - m]
                    acc = t if acc is None else acc + t
            part[f, u + 1] = acc
    b1, b4, b7 = part[1, 0], part[4, 0], part[7, 0]
    before = part[5, 0] - (part[3, 0] + b4)
    for u in range(units):
        b = [part[f, u + 1] for f in range(9)]
        a1e, a1o = b[0] + b1, b[2] - (b[0] + b[1])
        a2e, a2o = b[3] + b4, b[5] - (b[3] + b[4])
        a3e, a3o = b[6] + b7, b[8] - (b[6] + b[7])
        y = (a1e + before, a3e - (a1e + a2e), a1o + a2e, a3o - (a1o + a2o))
        b1, b4, b7, before = b[1], b[4], b[7], a2o
        for p in range(4):
            ybuf[pl.ds(4 * u + p, 8, stride=seg), :] = y[p]


def residual(x_ref, x_first, attn_ref, flags, marks, hid_ref, hid_first, cbuf, cbuf_first, gain, scale=None):
    def load(r, first):
        if not first:
            return hid_ref[pl.ds(hid_first + r, 16), :]
        on = [flags[flag] for upto, flag in reversed(marks) if r < upto][-1] > 0
        xf = x_ref[pl.ds(x_first + r, 16), :].astype(jnp.float32)
        hidden = jnp.where(on, xf + attn_ref[pl.ds(r, 16), :], xf)
        hid_ref[pl.ds(hid_first + r, 16), :] = hidden
        return hidden

    def store(r, value):
        value = value.astype(jnp.bfloat16).astype(jnp.float32)
        if scale is not None:
            value = value * scale
        for c in range(10):
            cbuf[c, pl.ds(cbuf_first + r, 16), :] = value[:, c * LANES : (c + 1) * LANES]

    norm_staged(load, store, marks[-1][0], gain)


def conv_rows(cbuf, w_ref, hid_ref, flags, first, units, comb, part, ybuf, out_ref, out_hbm, sems):
    count = 32 * units

    def lanes(c, comb, part, ybuf):
        cols = pl.ds(pl.multiple_of(c * LANES, LANES), LANES)
        conv_seg(cbuf, w_ref, c, cols, first, units, comb, part, ybuf)
        for r in range(0, count, 32):
            on = flags[3 + (first + r) // LANES] > 0
            half = ybuf[pl.ds(r, 32), :]
            hidden = hid_ref[pl.ds(first + r, 32), cols]
            out = jnp.where(on, hidden + (half + half * jnp.tanh(half)), hidden)
            out_ref[pl.ds(r, 32), cols] = out.astype(jnp.bfloat16)
        send(c).start()

    def two(i, carry):
        for j in range(2):
            lanes(2 * i + j, comb.at[j], part.at[j], ybuf.at[j])
        return carry

    def send(c):
        cols = pl.ds(pl.multiple_of(c * LANES, LANES), LANES)
        return pltpu.make_async_copy(
            out_ref.at[:, cols], out_hbm.at[pl.ds(first, count), cols], sems.at[c]
        )

    def finish(c, carry):
        send(c).wait()
        return carry

    lax.fori_loop(0, 5, two, 0)
    lax.fori_loop(0, 10, finish, 0)


def block_flags(segs, base):
    times = [base + (i - 3) * LANES for i in range(11)]
    lows = [jnp.int32(0)] * 11
    step = SEGS // 2
    while step:
        lows = [jnp.where(segs[0, lo + step] <= t, lo + step, lo) for lo, t in zip(lows, times)]
        step //= 2
    return [
        ((t >= 0) & (segs[0, lo] <= t) & (t < segs[1, lo])).astype(jnp.int32) for lo, t in zip(lows, times)
    ]


def kernel_a(segs, place, x_hbm, wq_hbm, wk_hbm, wv_hbm, wo_hbm, g1, g2, cw, out_hbm, q0, kv0, hid0, cin0, flags0,
             x, wqkv, wo, normed, qkv, heads, attn, hid, cbuf, out, comb, part, ybuf, sems, out_sems, table):
    feats = H * HS
    q, k, v = (qkv.at[:, pl.ds(i * feats, feats)] for i in range(3))
    copies = [
        pltpu.make_async_copy(x_hbm.at[pl.ds(b * ROWS, ROWS), :], x.at[pl.ds(b * ROWS, ROWS), :], sems.at[b])
        for b in range(4)
    ] + [
        pltpu.make_async_copy(wq_hbm, wqkv.at[:, pl.ds(0, feats)], sems.at[4]),
        pltpu.make_async_copy(wk_hbm, wqkv.at[:, pl.ds(feats, feats)], sems.at[5]),
        pltpu.make_async_copy(wv_hbm, wqkv.at[:, pl.ds(2 * feats, feats)], sems.at[6]),
        pltpu.make_async_copy(wo_hbm, wo, sems.at[7]),
    ]
    for i in (0, 4, 1, 2, 3, 5, 6, 7):
        copies[i].start()
    flags = block_flags(segs, place[0])
    for i in range(11):
        flags0[i] = flags[i]
    flags0[11] = jnp.minimum(place[0], 1)
    fill_weights(cw, table)
    gain1 = g1[...].reshape(1, -1)
    gain2 = g2[...].reshape(1, -1)
    def project(b, lo, hi):
        rows = pl.ds(b * ROWS, ROWS)
        qkv[rows, lo:hi] = jnp.dot(
            normed[rows, :], wqkv[:, lo:hi], preferred_element_type=jnp.float32
        ).astype(jnp.bfloat16)

    for b in range(4):
        copies[b].wait()
        norm_rows(x, normed, b * ROWS, ROWS, gain1)
        if b == 0:
            copies[4].wait()
        project(b, 0, 512)
    for i, lo, hi in ((5, 512, 2 * feats), (6, 2 * feats, 3 * feats)):
        copies[i].wait()
        for b in range(4):
            project(b, lo, hi)
    copies[7].wait()
    first = [
        pltpu.make_async_copy(qkv.at[pl.ds(0, ROWS), pl.ds(0, feats)], q0, sems.at[0]),
        pltpu.make_async_copy(qkv.at[pl.ds(0, ROWS), pl.ds(feats, 2 * feats)], kv0, sems.at[1]),
    ]
    for copy in first:
        copy.start()
    tri = tri_masks(ROWS)
    for b in range(1, 4):
        f = 3 + 2 * b
        bias = jnp.where(
            tri,
            bias_row(flags, [(128, f), (256, f + 1)]),
            bias_row(flags, [(128, f - 2), (256, f - 1)]),
        )
        attend(q, b * ROWS, k, v, (b - 1) * ROWS, ROWS, bias, tri, heads, (b - 1) * ROWS)
    attn[...] = jnp.dot(heads[...], wo[...], preferred_element_type=jnp.float32)
    for b in range(1, 4):
        f = 3 + 2 * b
        residual(x, b * ROWS, attn.at[pl.ds((b - 1) * ROWS, ROWS), :], flags, [(128, f), (256, f + 1)], hid, b * ROWS, cbuf, HALO + b * ROWS, gain2)
    rest = [
        pltpu.make_async_copy(hid.at[pl.ds(ROWS, SPLIT - ROWS), :], hid0, sems.at[3]),
        pltpu.make_async_copy(cbuf.at[:, pl.ds(HALO + ROWS, SPLIT - ROWS), :], cin0, sems.at[4]),
    ]
    for copy in rest:
        copy.start()
    conv_rows(cbuf, table, hid, flags, SPLIT, (1024 - SPLIT) // 32, comb, part, ybuf, out, out_hbm, out_sems)
    for copy in first + rest:
        copy.wait()


def kernel_b(flags, x_hbm, tail_hbm, wq_hbm, wk_hbm, wv_hbm, wo_hbm, g1, g2, cw, q0, kv0, hid0, cin0, _, out_hbm,
             tail, x, wqkv, wo, normed, q, kv, heads, attn, hid, halo_hid, cbuf, out, comb, part, ybuf, sems, out_sems, table):
    feats = H * HS
    k, v = (kv.at[:, pl.ds(i * feats, feats)] for i in range(2))
    copies = [
        pltpu.make_async_copy(tail_hbm, tail, sems.at[0]),
        pltpu.make_async_copy(wk_hbm, wqkv.at[:, pl.ds(feats, feats)], sems.at[1]),
        pltpu.make_async_copy(wv_hbm, wqkv.at[:, pl.ds(2 * feats, feats)], sems.at[2]),
        pltpu.make_async_copy(wq_hbm, wqkv.at[:, pl.ds(0, feats)], sems.at[3]),
        pltpu.make_async_copy(q0, q.at[pl.ds(HALO, ROWS), :], sems.at[4]),
        pltpu.make_async_copy(kv0, kv.at[pl.ds(EXTRA, ROWS), :], sems.at[5]),
        pltpu.make_async_copy(wo_hbm, wo, sems.at[6]),
        pltpu.make_async_copy(x_hbm.at[pl.ds(0, ROWS), :], x, sems.at[7]),
        pltpu.make_async_copy(hid0, hid.at[pl.ds(ROWS, SPLIT - ROWS), :], sems.at[8]),
        pltpu.make_async_copy(cin0, cbuf.at[:, pl.ds(HALO + ROWS, SPLIT - ROWS), :], sems.at[9]),
    ]
    for copy in copies:
        copy.start()
    fill_weights(cw, table)
    gain1 = g1[...].reshape(1, -1)
    gain2 = g2[...].reshape(1, -1)
    copies[0].wait()
    norm_rows(tail, normed, 0, EXTRA, gain1)
    for i, lo, hi in ((1, 0, 512), (2, 512, 2 * feats)):
        copies[i].wait()
        kv[pl.ds(0, EXTRA), lo:hi] = jnp.dot(
            normed[...], wqkv[:, feats + lo : feats + hi], preferred_element_type=jnp.float32
        ).astype(jnp.bfloat16)
    copies[3].wait()
    q[pl.ds(0, HALO), :] = jnp.dot(
        normed[pl.ds(CTX, HALO), :], wqkv[:, :feats], preferred_element_type=jnp.float32
    ).astype(jnp.bfloat16)
    copies[4].wait()
    copies[5].wait()
    small = tri_masks(HALO)
    bias = jnp.where(
        small, bias_row(flags, [(HALO, 2)]), bias_row(flags, [(HALO, 0), (HALO + 128, 1), (256, 2)])
    )
    attend(q, 0, k, v, 0, HALO, bias, small, heads, 0)
    tri = tri_masks(ROWS)
    bias = jnp.where(
        tri, bias_row(flags, [(128, 3), (256, 4)]), bias_row(flags, [(128, 1), (256, 2)])
    )
    attend(q, HALO, k, v, HALO, ROWS, bias, tri, heads, HALO)
    for copy in copies[6:]:
        copy.wait()
    attn[...] = jnp.dot(heads[...], wo[...], preferred_element_type=jnp.float32)
    keep = jnp.where(flags[11] > 0, 1.0, 0.0)
    residual(tail, CTX, attn, flags, [(HALO, 2)], halo_hid, 0, cbuf, 0, gain2, keep)
    residual(x, 0, attn.at[pl.ds(HALO, ROWS), :], flags, [(128, 3), (256, 4)], hid, 0, cbuf, HALO, gain2)
    conv_rows(cbuf, table, hid, flags, 0, SPLIT // 32, comb, part, ybuf, out, out_hbm, out_sems)


def per_device(frames, segments, ln_gain, w_query, w_key, w_value, w_out, conv_gain, conv_weight):
    x = frames[0]
    count, width = x.shape
    feats = H * HS
    peers = lax.axis_size("tm")
    me = lax.axis_index("tm")
    tail = lax.ppermute(x[count - EXTRA :], "tm", [(i, i + 1) for i in range(peers - 1)])
    place = (me * count).reshape(1).astype(jnp.int32)
    segs = segments[0].T
    hbm = pl.BlockSpec(memory_space=pl.ANY)
    vmem = pl.BlockSpec(memory_space=pltpu.VMEM)
    smem = pl.BlockSpec(memory_space=pltpu.SMEM)
    bf16, f32 = jnp.bfloat16, jnp.float32
    late = count - SPLIT
    out, q0, kv0, hid0, cin0, flags = pl.pallas_call(
        kernel_a,
        in_specs=[smem, smem, hbm, hbm, hbm, hbm, hbm, vmem, vmem, vmem],
        out_specs=[hbm] * 5 + [smem],
        out_shape=[
            jax.ShapeDtypeStruct((count, width), bf16),
            jax.ShapeDtypeStruct((ROWS, feats), bf16),
            jax.ShapeDtypeStruct((ROWS, 2 * feats), bf16),
            jax.ShapeDtypeStruct((SPLIT - ROWS, width), f32),
            jax.ShapeDtypeStruct((10, SPLIT - ROWS, LANES), f32),
            jax.ShapeDtypeStruct((12,), jnp.int32),
        ],
        scratch_shapes=[
            pltpu.VMEM((count, width), bf16),
            pltpu.VMEM((width, 3 * feats), bf16),
            pltpu.VMEM((feats, width), bf16),
            pltpu.VMEM((count, width), bf16),
            pltpu.VMEM((count, 3 * feats), bf16),
            pltpu.VMEM((count - ROWS, feats), bf16),
            pltpu.VMEM((count - ROWS, width), f32),
            pltpu.VMEM((count, width), f32),
            pltpu.VMEM((10, HALO + count, LANES), f32),
            pltpu.VMEM((late, width), bf16),
            pltpu.VMEM((2, 9, late // 32 + 8, 8, LANES), f32),
            pltpu.VMEM((2, 9, late // 32 + 1, 8, LANES), f32),
            pltpu.VMEM((2, late, LANES), f32),
            pltpu.SemaphoreType.DMA((8,)),
            pltpu.SemaphoreType.DMA((10,)),
            pltpu.VMEM((72, width), f32),
        ],
        compiler_params=pltpu.CompilerParams(vmem_limit_bytes=63 << 20),
        cost_estimate=pl.CostEstimate(flops=12_000_000_000, bytes_accessed=11_000_000, transcendentals=4_000_000),
        name="own_rows",
    )(segs, place, x, w_query, w_key, w_value, w_out, ln_gain, conv_gain, conv_weight)
    out = pl.pallas_call(
        kernel_b,
        in_specs=[smem, hbm, pl.BlockSpec(memory_space=pltpu.HBM)] + [hbm] * 4 + [vmem] * 3 + [hbm] * 5,
        out_specs=hbm,
        out_shape=jax.ShapeDtypeStruct((count, width), bf16),
        input_output_aliases={14: 0},
        scratch_shapes=[
            pltpu.VMEM((EXTRA, width), bf16),
            pltpu.VMEM((ROWS, width), bf16),
            pltpu.VMEM((width, 3 * feats), bf16),
            pltpu.VMEM((feats, width), bf16),
            pltpu.VMEM((EXTRA, width), bf16),
            pltpu.VMEM((EXTRA, feats), bf16),
            pltpu.VMEM((EXTRA + ROWS, 2 * feats), bf16),
            pltpu.VMEM((EXTRA, feats), bf16),
            pltpu.VMEM((EXTRA, width), f32),
            pltpu.VMEM((SPLIT, width), f32),
            pltpu.VMEM((HALO, width), f32),
            pltpu.VMEM((10, HALO + SPLIT, LANES), f32),
            pltpu.VMEM((SPLIT, width), bf16),
            pltpu.VMEM((2, 9, SPLIT // 32 + 8, 8, LANES), f32),
            pltpu.VMEM((2, 9, SPLIT // 32 + 1, 8, LANES), f32),
            pltpu.VMEM((2, SPLIT, LANES), f32),
            pltpu.SemaphoreType.DMA((10,)),
            pltpu.SemaphoreType.DMA((10,)),
            pltpu.VMEM((72, width), f32),
        ],
        compiler_params=pltpu.CompilerParams(vmem_limit_bytes=63 << 20),
        cost_estimate=pl.CostEstimate(flops=4_000_000_000, bytes_accessed=9_000_000, transcendentals=1_000_000),
        name="first_rows",
    )(flags, x, tail, w_query, w_key, w_value, w_out, ln_gain, conv_gain, conv_weight, q0, kv0, hid0, cin0, out)
    return out[None]


def solution(mesh):
    in_specs = (P("rec", "tm", None), P("rec", None, None), P(), P(), P(), P(), P(), P(), P())
    out_specs = P("rec", "tm", None)
    return jax.shard_map(
        per_device, mesh=mesh, in_specs=in_specs, out_specs=out_specs, check_vma=False
    )
```
